128 devices in a mesh: clip: 64 (over x, z, y_lo, core), space: 2 (over y_hi).
Axes of the slice: x: 4, y: 4 (y_hi: 2, y_lo: 2; y = y_hi * 2 + y_lo), z: 4, core: 2. Of those that a mesh axis runs over, the one named last changes fastest.
Arguments:
- latent: bfloat16 [1024, 96, 1280], P('clip', 'space'), may hold values from -160 to 160
- gn_gain: float32 [1280], replicated, may hold values from 0.1 to 1.9
- gn_bias: float32 [1280], replicated, may hold values from -3 to 3
- w_query: bfloat16 [1280, 1280], replicated, may hold values from -2 to 2
- w_key: bfloat16 [1280, 1280], replicated, may hold values from -2 to 2
- w_value: bfloat16 [1280, 1280], replicated, may hold values from -0.15625 to 0.15625
- w_out: bfloat16 [1280, 1280], replicated, may hold values from -0.15625 to 0.15625
- out_bias: float32 [1280], replicated, may hold values from -3 to 3
- context_frames: int32 [64, 1], P('clip'), may hold values from 0 to 15
Outputs:
- mixed: bfloat16 [1024, 96, 1280], P('clip', 'space')
The draws below stay inside these ranges and needn't reach their ends.
All inputs are finite; a program needn't handle non-finite values.
Results may differ from the reference program's by a relative error of at most 0.0034.
The reference program's roundings to bfloat16 on the way (of `normed`, `weights` and `attended`) count: a program that leaves them out, or rounds other values in their place, can miss the bound.
Values may be sent and summed in bfloat16 or wider, within the bound.
A program may use at most 192 MiB of HBM per device.

```python
import math
import jax
import jax.numpy as jnp
from jax import lax

C = 1280
HEADS = 20
HEAD_DIM = 64
GROUPS = 32
FRAMES = 16
EDGE = 4
CTX = 1
POS = 96
TOTAL_FRAMES = 1024
N_CLIP = 64


def shared_base(key):
    return jnp.clip(jax.random.normal(key, (C, C), jnp.float32), -4.0, 4.0) / math.sqrt(C)


def draw_w_query(key, part):
    base = shared_base(key)
    return base.astype(jnp.bfloat16)


def draw_w_key(key, part):
    key = jax.random.fold_in(key, 7)
    other = shared_base(key)
    return other.astype(jnp.bfloat16)


def draw_latent(key, part):
    key = jax.random.fold_in(key, 3)
    first, second, third, fourth = jax.random.split(key, 4)
    place = jnp.arange(POS, dtype=jnp.float32) / max(POS - 1, 1)
    ramp = jnp.power(10.0, place) * jax.random.uniform(second, (POS,), jnp.float32, 0.7, 1.4)
    frame_scale = jnp.exp(jax.random.uniform(third, (TOTAL_FRAMES,), jnp.float32, math.log(0.5), math.log(2.0)))
    scale = frame_scale[:, None, None] * ramp[None, :, None]
    noise = jnp.clip(jax.random.normal(first, (TOTAL_FRAMES, POS, C), jnp.float32), -4.0, 4.0)
    noise = noise + jax.random.uniform(fourth, (C,), jnp.float32, 0.4, 1.0)
    return (noise * scale).astype(jnp.bfloat16)


def plant(array, own_key, least, largest):
    extent = array.shape
    spot = [jax.random.randint(jax.random.fold_in(own_key, axis), (), 0, extent[axis]) for axis in range(len(extent))]
    array = array.at[tuple(spot)].set(least)
    longest = extent.index(max(extent))
    spot[longest] = (spot[longest] + 1) % extent[longest]
    return array.at[tuple(spot)].set(largest)


def gaussian(stream_key, dims, scale, most, held_as=jnp.bfloat16):
    array = scale * jax.random.normal(stream_key, dims, jnp.float32)
    return jnp.clip(array, min=-most, max=most).astype(held_as)


def setup_inputs(seed: int = 0) -> dict:
    splits = jax.random.split(jax.random.key(seed), 10)
    return {
        "latent": draw_latent(jax.random.fold_in(splits[9], 71), 0),
        "gn_gain": jnp.clip(1.0 + 0.18 * jax.random.normal(splits[1], (C,), jnp.float32), 0.1, 1.9),
        "gn_bias": gaussian(splits[2], (C,), 0.5, 3.0, jnp.float32),
        "w_query": draw_w_query(jax.random.fold_in(splits[9], 71), 0),
        "w_key": draw_w_key(jax.random.fold_in(splits[9], 71), 0),
        "w_value": gaussian(splits[5], (C, C), C ** -0.5, 0.15625),
        "w_out": gaussian(splits[6], (C, C), C ** -0.5, 0.15625),
        "out_bias": gaussian(splits[7], (C,), 0.5, 3.0, jnp.float32),
        "context_frames": plant(jax.random.randint(splits[8], (N_CLIP, CTX), 0, FRAMES), jax.random.fold_in(splits[8], 1), 0, FRAMES - 1).astype(jnp.int32),
    }


EPS = 1e-06

def project(rows_in, weight):
    flat = rows_in.reshape(-1, rows_in.shape[-1])
    out = jnp.dot(flat, weight, preferred_element_type=jnp.float32).astype(jnp.bfloat16)
    return out.reshape(rows_in.shape[:-1] + (weight.shape[1],))

def attend(query, keys, values, valid):
    frames, rows, width = query.shape
    count = keys.shape[0]
    qh = query.reshape(frames, rows, HEADS, HEAD_DIM).astype(jnp.float32)
    kh = keys.reshape(count, rows, HEADS, HEAD_DIM).astype(jnp.float32)
    vh = values.reshape(count, rows, HEADS, HEAD_DIM).astype(jnp.float32)
    scores = jnp.einsum('fphd,kphd->phfk', qh, kh) * (1.0 / math.sqrt(HEAD_DIM))
    scores = jnp.where(valid[None, None, None, :], scores, -jnp.inf)
    top = lax.optimization_barrier(jnp.max(scores, axis=-1, keepdims=True))
    expo = jnp.exp(scores - top)
    weights = (expo / lax.optimization_barrier(jnp.sum(expo, axis=-1, keepdims=True))).astype(jnp.bfloat16)
    out = jnp.einsum('phfk,kphd->fphd', weights.astype(jnp.float32), vh)
    return out.reshape(frames, rows, width).astype(jnp.bfloat16)

def reference(latent, gn_gain, gn_bias, w_query, w_key, w_value, w_out, out_bias, context_frames):
    per = C // GROUPS
    x = latent.astype(jnp.float32).reshape(N_CLIP, FRAMES, POS, GROUPS, per)
    mean = lax.optimization_barrier(jnp.mean(x, axis=(1, 2, 4), keepdims=True))
    var = lax.optimization_barrier(jnp.mean((x - mean) * (x - mean), axis=(1, 2, 4), keepdims=True))
    normed = ((x - mean) * lax.rsqrt(var + EPS)).reshape(TOTAL_FRAMES, POS, C)
    normed = (normed * gn_gain + gn_bias).astype(jnp.bfloat16)
    query = project(normed, w_query)
    key = project(normed, w_key)
    value = project(normed, w_value)
    picks = (jnp.arange(N_CLIP, dtype=jnp.int32)[:, None] * FRAMES + context_frames.astype(jnp.int32)).reshape(-1)
    context_k = jnp.take(key, picks, axis=0)
    context_v = jnp.take(value, picks, axis=0)

    def one_clip(index):
        start = (index * FRAMES).astype(jnp.int32)
        left = jnp.maximum(start - EDGE, 0).astype(jnp.int32)
        right = jnp.minimum(start + FRAMES, TOTAL_FRAMES - EDGE).astype(jnp.int32)
        q_local = lax.dynamic_slice_in_dim(query, start, FRAMES, 0)
        keys = jnp.concatenate([lax.dynamic_slice_in_dim(key, left, EDGE, 0), lax.dynamic_slice_in_dim(key, start, FRAMES, 0), lax.dynamic_slice_in_dim(key, right, EDGE, 0), context_k], axis=0)
        values = jnp.concatenate([lax.dynamic_slice_in_dim(value, left, EDGE, 0), lax.dynamic_slice_in_dim(value, start, FRAMES, 0), lax.dynamic_slice_in_dim(value, right, EDGE, 0), context_v], axis=0)
        valid = jnp.concatenate([jnp.full((EDGE,), index > 0), jnp.ones((FRAMES,), bool), jnp.full((EDGE,), index < N_CLIP - 1), jnp.ones((N_CLIP * CTX,), bool)])
        return attend(q_local, keys, values, valid)
    attended = lax.map(one_clip, jnp.arange(N_CLIP, dtype=jnp.int32)).reshape(TOTAL_FRAMES * POS, C)
    branch = jnp.dot(attended, w_out, preferred_element_type=jnp.float32).reshape(TOTAL_FRAMES, POS, C)
    return (latent.astype(jnp.float32) + branch + out_bias).astype(jnp.bfloat16)
```

```python
import numpy as np

import jax
import jax.numpy as jnp
from jax import lax
from jax.experimental import pallas as pl
from jax.experimental.pallas import tpu as pltpu
from jax.sharding import PartitionSpec as P

C = 1280
HEAD_DIM = 64
GROUPS = 32
FRAMES = 16
EDGE = 4
EPS = 1e-06
ROWS = 48
HALF = 24
KEYS = 112
TILE = 256
TILES = C // TILE
MESH = pl.DeviceIdType.MESH
F32, BF16 = jnp.float32, jnp.bfloat16


def swap_matrix(outer, inner, blocks=1):
    n = outer * inner
    m = np.zeros((n, n), np.float32)
    for i in range(outer):
        for j in range(inner):
            m[j * outer + i, i * inner + j] = 1
    return m


def edge_merge():
    m = np.zeros((192, 192), np.float32)
    for side in range(2):
        for p in range(HALF):
            for f in range(EDGE):
                m[p * 8 + side * 4 + f, side * 96 + p * 4 + f] = 1
    return m


SWAP16 = swap_matrix(16, 16)
SWAP8 = swap_matrix(16, 8)
EDGE_OUT = swap_matrix(EDGE, ROWS)
EDGE_IN = edge_merge()
GROUP_OF = np.zeros((C, 128), np.float32)
GROUP_OF[np.arange(C), np.arange(C) // (C // GROUPS)] = 1
HEAD_MASK = np.zeros((128, TILE), np.float32)
for _h in range(4):
    HEAD_MASK[_h * 32 : _h * 32 + 32, _h * 64 : _h * 64 + 64] = 1


def dot(a, b):
    return jnp.dot(a, b, preferred_element_type=F32)


def exact_dot(a, b):
    return jnp.dot(a, b, preferred_element_type=F32, precision=lax.Precision.HIGHEST)


def slot_of(i, j, s):
    return j * 8 + i * 2 + s


def kernel(
    latent, gain, shift, wq, wk, wv, wo, out_bias, picks, swap16, swap8, edge_out, edge_in, group_of, group_to, head_mask,
    out,
    lat, normed, turned, sib, ctx, xc, edge_tx, edge_rx, edge_x, query, kv, att, att_tx, result, w, w_out,
    s16, s8, e_out, e_in, g_of, g_to, h_mask, stat_tx, stat_rx, pick_own, pick_tx, pick_rx, mask,
    load_sem, send_sem, recv_sem, misc_tx, misc_rx, att_sem_tx, att_sem_rx, store_sem,
):
    clip = lax.axis_index("clip")
    space = lax.axis_index("space")
    core = clip % 2
    y = (clip // 2) % 2
    z = (clip // 4) % 4
    x = clip // 16
    chip = clip // 2

    def device(x, z, y, core):
        return (((x * 4 + z) * 2 + y) * 2 + core, space)

    def along(first, step):
        on_x = (1 - core) if first else core
        return device((x + step * on_x) % 4, (z + step * (1 - on_x)) % 4, y, core)

    a_up, a_down = along(True, 1), along(True, 3)
    b_up, b_down = along(False, 1), along(False, 3)
    y_pair = device(x, z, 1 - y, core)
    sibling = (clip + 1 - 2 * core, space)
    other_space = (clip, 1 - space)
    edge_chip = (chip + 2 * core + 31) % 32
    edge_to = [(edge_chip * 2, space), (edge_chip * 2 + 1, space)]
    edge_from = [(((chip + 31) % 32) * 2 + 1, space), (((chip + 1) % 32) * 2, space)]

    barrier = pltpu.get_barrier_semaphore()
    greet = [a_up, a_down, b_up, b_down, y_pair, sibling, other_space] + edge_to + edge_from
    for other in greet:
        pl.semaphore_signal(barrier, inc=1, device_id=other, device_id_type=MESH)

    loads = [
        pltpu.make_async_copy(src, dst, load_sem.at[n])
        for n, (src, dst) in enumerate(
            [
                (latent, lat),
                (group_of, g_of),
                (group_to, g_to),
                (swap16, s16),
                (edge_out, e_out),
                (wq, w.at[0]),
                (wk, w.at[1]),
                (wv, w.at[2]),
                (swap8, s8),
                (edge_in, e_in),
                (head_mask, h_mask),
                (wo, w_out),
            ]
        )
    ]
    for copy in loads:
        copy.start()

    row = lax.broadcasted_iota(jnp.int32, (48, 128), 0)
    lane = lax.broadcasted_iota(jnp.int32, (48, 128), 1)
    q_clip = (((lane >> 4) & 1) + core) & 1
    k_clip = (((row >> 4) & 1) + core) & 1
    frame = row & 15
    local = (row < 32) & (
        (k_clip == q_clip)
        | ((q_clip == 0) & (frame < EDGE))
        | ((q_clip == 1) & (frame >= FRAMES - EDGE))
    )
    left = (row >= 32) & (row < 36) & (q_clip == 0) & (chip > 0)
    right = (row >= 36) & (row < 40) & (q_clip == 1) & (chip < 31)
    mask[...] = jnp.where(local | left | right, 0.0, -jnp.inf).astype(F32)

    loads[0].wait()

    def add_rows(f, acc):
        v = lat[f].astype(F32)
        for r in range(ROWS // 8):
            acc = acc + v[8 * r : 8 * r + 8]
        return acc

    total = lax.fori_loop(0, FRAMES, add_rows, jnp.zeros((8, C), F32))
    loads[1].wait()
    loads[2].wait()
    count = FRAMES * ROWS * (C // GROUPS)
    mean_here = jnp.sum(exact_dot(total, g_of[...]), axis=0, keepdims=True) * (1.0 / count)
    mean_here = jnp.broadcast_to(mean_here, (8, 128))
    wide = exact_dot(mean_here, g_to[...])

    def add_squares(f, acc):
        v = lat[f].astype(F32)
        for r in range(ROWS // 8):
            d = v[8 * r : 8 * r + 8] - wide
            acc = acc + d * d
        return acc

    squares = lax.fori_loop(0, FRAMES, add_squares, jnp.zeros((8, C), F32))
    dev_here = jnp.sum(exact_dot(squares, g_of[...]), axis=0, keepdims=True)
    dev_here = jnp.broadcast_to(dev_here, (8, 128))
    first_row = lax.broadcasted_iota(jnp.int32, (8, 128), 0) == 0
    stat_tx[...] = jnp.where(first_row, mean_here, dev_here)

    pl.semaphore_wait(barrier, len(greet))

    def misc(n, src, dst, to):
        return pltpu.make_async_remote_copy(
            src_ref=src, dst_ref=dst, send_sem=misc_tx.at[n], recv_sem=misc_rx.at[n], device_id=to, device_id_type=MESH
        )

    stats = misc(0, stat_tx, stat_rx, other_space)
    stats.start()
    stats.wait_recv()
    mean_there = stat_rx[0:1]
    dev_there = stat_rx[1:2]
    gap = mean_here[0:1] - mean_there
    mean = 0.5 * (mean_here[0:1] + mean_there)
    var = (dev_here[0:1] + dev_there + gap * gap * (0.5 * count)) * (0.5 / count)
    scale = lax.rsqrt(var + EPS)
    both = jnp.where(first_row, jnp.broadcast_to(mean, (8, 128)), jnp.broadcast_to(scale, (8, 128)))
    both = exact_dot(both, g_to[...])
    mean_c = both[0:1]
    gain_c = both[1:2] * gain[...]
    shift_c = shift[...]

    def norm(v):
        return ((v.astype(F32) - mean_c) * gain_c + shift_c).astype(BF16)

    picked = norm(lat[picks[0, 0]]).astype(F32)
    low, high = picked[:HALF], picked[HALF:]
    pick_own[...] = jnp.where(core == 0, low, high)
    pick_tx[...] = jnp.where(core == 0, high, low)
    swap_pick = misc(1, pick_tx, pick_rx, sibling)
    swap_pick.start()

    def normalize(f, _):
        normed[f] = norm(lat[f])
        return 0

    lax.fori_loop(0, FRAMES, normalize, 0)

    swap_pick.wait_recv()
    for g in range(3):
        pair = jnp.concatenate([pick_own[8 * g : 8 * g + 8], pick_rx[8 * g : 8 * g + 8]], axis=0)
        ctx[g, 0:16, :] = pair.astype(BF16)

    def hop(i, j, s):
        if j == 0:
            if i == 0:
                src, to = (0, 0, 0), y_pair
            elif i == 1:
                src, to = (0, 0, s), a_up
            elif i == 2:
                src, to = (0, 0, s), a_down
            else:
                src, to = ((1, 0, 0), a_up) if s == 0 else ((2, 0, 1), a_down)
        elif j == 1:
            src, to = (i, 0, s), b_up
        elif j == 2:
            src, to = (i, 0, s), b_down
        else:
            src, to = ((i, 1, 0), b_up) if s == 0 else ((i, 2, 1), b_down)
        n, dst = slot_of(*src), slot_of(i, j, s)
        return pltpu.make_async_remote_copy(
            src_ref=ctx.at[:, 16 * n : 16 * n + 16, :],
            dst_ref=ctx.at[:, 16 * dst : 16 * dst + 16, :],
            send_sem=send_sem.at[dst],
            recv_sem=recv_sem.at[dst],
            device_id=to,
            device_id_type=MESH,
        )

    def start(*slots):
        for slot in slots:
            hop(*slot).start()

    start((0, 0, 1), (1, 0, 0), (2, 0, 0), (0, 1, 0), (0, 2, 0))

    loads[3].wait()

    def turn(q, _):
        rows = normed[:, pl.ds(pl.multiple_of(q * 16, 16), 16), :].reshape(256, C)
        turned[pl.ds(q * 16, 16)] = dot(s16[...], rows).astype(BF16).reshape(16, 16, C)
        return 0

    lax.fori_loop(0, 3, turn, 0)
    swap_rows = misc(2, turned.at[pl.ds(HALF * (1 - core), HALF)], sib, sibling)
    swap_rows.start()
    loads[4].wait()
    edge_rows = normed[pl.ds(12 * core, EDGE)].reshape(EDGE * ROWS, C)
    edge_tx[...] = dot(e_out[...], edge_rows).astype(BF16).reshape(2, 96, C)
    edge_sends = [
        pltpu.make_async_remote_copy(
            src_ref=edge_tx.at[k],
            dst_ref=edge_rx.at[1 - core],
            send_sem=misc_tx.at[3 + k],
            recv_sem=misc_rx.at[3 + 1 - core],
            device_id=edge_to[k],
            device_id_type=MESH,
        )
        for k in range(2)
    ]
    for copy in edge_sends:
        copy.start()

    def edge_arrived(n):
        pltpu.make_async_copy(edge_rx.at[n], edge_rx.at[n], misc_rx.at[3 + n]).wait()

    def pass_on(arrived, *slots):
        def act():
            hop(*arrived).wait_recv()
            start(*slots)

        return act

    def forward(i, s):
        return pass_on((i, 1, 0), (i, 3, 0)) if s == 0 else pass_on((i, 2, 1), (i, 3, 1))

    def run(acts, t):
        for when, act in acts:
            pl.when(t == when)(act)

    def project_query(rows, at, acts=()):
        def step(n, _):
            run(acts, n)
            cols = pl.ds(pl.multiple_of(n * TILE, TILE), TILE)
            res = dot(rows(), w[0, :, cols]) * (HEAD_DIM**-0.5)
            query[:, at : at + 16, cols] = res.astype(BF16).reshape(HALF, 16, TILE)
            return 0

        lax.fori_loop(0, TILES, step, 0)

    def project_kv(rows, at, acts=()):
        def step(t, _):
            run(acts, t)
            m = t // TILES
            cols = pl.ds(pl.multiple_of((t % TILES) * TILE, TILE), TILE)
            res = dot(rows(), w[1 + m, :, cols])
            kv[m, :, at : at + 16, cols] = res.astype(BF16).reshape(HALF, 16, TILE)
            return 0

        lax.fori_loop(0, 2 * TILES, step, 0)

    def own_rows():
        return turned[pl.ds(HALF * core, HALF)].reshape(HALF * 16, C)

    def sib_rows():
        return sib[...].reshape(HALF * 16, C)

    def ctx_rows():
        return xc[...]

    def gather_ctx(j):
        def one(g, _):
            rows = dot(s8[...], ctx[g, 128 * j : 128 * j + 128, :])
            xc[pl.ds(pl.multiple_of(g * 128, 128), 128)] = rows.astype(BF16)
            return 0

        lax.fori_loop(0, 3, one, 0)

    loads[5].wait()
    project_query(
        own_rows, 0,
        [(3, pass_on((0, 0, 1), (1, 0, 1), (2, 0, 1), (0, 1, 1), (0, 2, 1)))],
    )
    loads[6].wait()
    loads[7].wait()
    project_kv(
        own_rows, 64,
        [
            (1, pass_on((1, 0, 0), (3, 0, 0), (1, 1, 0), (1, 2, 0))),
            (2, pass_on((2, 0, 0), (2, 1, 0), (2, 2, 0))),
            (6, pass_on((2, 0, 1), (3, 0, 1), (2, 1, 1), (2, 2, 1))),
            (7, pass_on((1, 0, 1), (1, 1, 1), (1, 2, 1))),
        ],
    )
    swap_rows.wait_recv()
    project_query(
        sib_rows, 16,
        [(1, pass_on((3, 0, 0), (3, 1, 0), (3, 2, 0))), (4, pass_on((3, 0, 1), (3, 1, 1), (3, 2, 1)))],
    )
    project_kv(
        sib_rows, 80,
        [(1, forward(0, 0)), (3, forward(0, 1)), (5, forward(1, 0)), (7, forward(2, 0)), (9, forward(2, 1))],
    )
    loads[8].wait()
    gather_ctx(0)
    project_kv(ctx_rows, 0, [(1, forward(1, 1)), (4, forward(3, 0)), (7, forward(3, 1))])
    for i in range(4):
        hop(i, 1, 1).wait_recv()
        hop(i, 2, 0).wait_recv()
    gather_ctx(1)
    project_kv(ctx_rows, 16)
    gather_ctx(2)
    project_kv(ctx_rows, 32)

    loads[9].wait()
    edge_arrived(0)
    edge_arrived(1)
    edge_x[...] = dot(e_in[...], edge_rx[...].reshape(192, C)).astype(BF16)

    def edge_step(t, _):
        m = t // TILES
        cols = pl.ds(pl.multiple_of((t % TILES) * TILE, TILE), TILE)
        res = dot(edge_x[...], w[1 + m, :, cols]).reshape(HALF, 8, TILE)
        res = jnp.concatenate([res, jnp.zeros((HALF, 8, TILE), F32)], axis=1)
        kv[m, :, 96:112, cols] = res.astype(BF16)
        return 0

    lax.fori_loop(0, 2 * TILES, edge_step, 0)

    for i in range(4):
        for s in range(2):
            hop(i, 3, s).wait_recv()
    gather_ctx(3)
    project_kv(ctx_rows, 48)

    loads[10].wait()
    loads[11].wait()

    def send_att(c):
        there = pl.ds(HALF * core + 8 * c, 8)
        return pltpu.make_async_remote_copy(
            src_ref=att_tx.at[8 * c : 8 * c + 8],
            dst_ref=att.at[there],
            send_sem=att_sem_tx.at[c],
            recv_sem=att_sem_rx.at[c],
            device_id=sibling,
            device_id_type=MESH,
        )

    def attend(p, _):
        half = lax.broadcasted_iota(jnp.int32, (32, 128), 1) < HEAD_DIM
        for h in range(TILES):
            cols = slice(h * TILE, (h + 1) * TILE)
            q = query[p, :, cols]
            q = jnp.concatenate([q] * 4, axis=0) * h_mask[...]
            scores = lax.dot_general(
                kv[0, p, :, cols], q, (((1,), (1,)), ((), ())), preferred_element_type=F32
            )
            scores = jnp.concatenate([scores[:64], scores[64:] + mask[...]], axis=0)
            top = jnp.max(scores, axis=0, keepdims=True)
            expo = jnp.exp(scores - top)
            share = 1.0 / jnp.sum(expo, axis=0, keepdims=True)
            weights = (expo * share).astype(BF16)
            mixed = lax.dot_general(
                weights, kv[1, p, :, cols], (((0,), (0,)), ((), ())), preferred_element_type=F32
            )
            for t in range(2):
                lanes = slice(128 * t, 128 * t + 128)
                lo = mixed[64 * t : 64 * t + 32, lanes]
                hi = mixed[64 * t + 32 : 64 * t + 64, lanes]
                both = jnp.where(half, lo, hi).astype(BF16)
                to = slice(h * TILE + 128 * t, h * TILE + 128 * t + 128)
                att[HALF * core + p, :, to] = both[:16]
                att_tx[p, :, to] = both[16:]
        return 0

    for c in range(3):
        lax.fori_loop(8 * c, 8 * c + 8, attend, 0)
        send_att(c).start()
    for c in range(3):
        there = pl.ds(HALF * (1 - core) + 8 * c, 8)
        pltpu.make_async_copy(att.at[there], att.at[there], att_sem_rx.at[c]).wait()

    def turn_back(q, _):
        rows = att[pl.ds(q * 16, 16)].reshape(256, C)
        turned_rows = dot(s16[...], rows).astype(BF16)
        normed[:, pl.ds(pl.multiple_of(q * 16, 16), 16), :] = turned_rows.reshape(16, 16, C)
        return 0

    lax.fori_loop(0, 3, turn_back, 0)

    def project_out(n, _):
        cols = pl.ds(pl.multiple_of(n * TILE, TILE), TILE)
        res = dot(normed[...].reshape(FRAMES * ROWS, C), w_out[:, cols])
        res = lat[:, :, cols].astype(F32) + res.reshape(FRAMES, ROWS, TILE) + out_bias[:, cols].reshape(1, 1, TILE)
        result[:, :, cols] = res.astype(BF16)
        return 0

    lax.fori_loop(0, TILES, project_out, 0)
    store = pltpu.make_async_copy(result, out, store_sem)
    store.start()

    stats.wait_send()
    swap_pick.wait_send()
    swap_rows.wait_send()
    for copy in edge_sends:
        copy.wait_send()
    for j in range(4):
        for i in range(4):
            for s in range(2):
                if (i, j, s) != (0, 0, 0):
                    hop(i, j, s).wait_send()
    for c in range(3):
        send_att(c).wait_send()
    store.wait()


def local(latent, gn_gain, gn_bias, w_query, w_key, w_value, w_out, out_bias, context_frames):
    consts = [
        jnp.asarray(SWAP16, BF16),
        jnp.asarray(SWAP8, BF16),
        jnp.asarray(EDGE_OUT, BF16),
        jnp.asarray(EDGE_IN, BF16),
        jnp.asarray(GROUP_OF, F32),
        jnp.asarray(GROUP_OF.T.copy(), F32),
        jnp.asarray(HEAD_MASK, BF16),
    ]
    any_ = pl.BlockSpec(memory_space=pl.ANY)
    vmem = pl.BlockSpec(memory_space=pltpu.VMEM)
    smem = pl.BlockSpec(memory_space=pltpu.SMEM)
    dma = pltpu.SemaphoreType.DMA
    return pl.pallas_call(
        kernel,
        out_shape=jax.ShapeDtypeStruct((FRAMES, ROWS, C), BF16),
        in_specs=[any_, vmem, vmem, any_, any_, any_, any_, vmem, smem] + [any_] * 7,
        out_specs=any_,
        scratch_shapes=[
            pltpu.VMEM((FRAMES, ROWS, C), BF16),
            pltpu.VMEM((FRAMES, ROWS, C), BF16),
            pltpu.VMEM((ROWS, FRAMES, C), BF16),
            pltpu.VMEM((HALF, FRAMES, C), BF16),
            pltpu.VMEM((3, 512, C), BF16),
            pltpu.VMEM((HALF * 16, C), BF16),
            pltpu.VMEM((2, 96, C), BF16),
            pltpu.VMEM((2, 96, C), BF16),
            pltpu.VMEM((192, C), BF16),
            pltpu.VMEM((HALF, 32, C), BF16),
            pltpu.VMEM((2, HALF, KEYS, C), BF16),
            pltpu.VMEM((ROWS, FRAMES, C), BF16),
            pltpu.VMEM((HALF, FRAMES, C), BF16),
            pltpu.VMEM((FRAMES, ROWS, C), BF16),
            pltpu.VMEM((3, C, C), BF16),
            pltpu.VMEM((C, C), BF16),
            pltpu.VMEM((256, 256), BF16),
            pltpu.VMEM((128, 128), BF16),
            pltpu.VMEM((192, 192), BF16),
            pltpu.VMEM((192, 192), BF16),
            pltpu.VMEM((C, 128), F32),
            pltpu.VMEM((128, C), F32),
            pltpu.VMEM((128, TILE), BF16),
            pltpu.VMEM((8, 128), F32),
            pltpu.VMEM((8, 128), F32),
            pltpu.VMEM((HALF, C), F32),
            pltpu.VMEM((HALF, C), F32),
            pltpu.VMEM((HALF, C), F32),
            pltpu.VMEM((48, 128), F32),
            dma((12,)),
            dma((32,)),
            dma((32,)),
            dma((5,)),
            dma((5,)),
            dma((3,)),
            dma((3,)),
            dma,
        ],
        compiler_params=pltpu.CompilerParams(
            collective_id=0, has_side_effects=True, vmem_limit_bytes=60 * 1024 * 1024
        ),
        cost_estimate=pl.CostEstimate(flops=25 * 10**9, bytes_accessed=18 * 10**6, transcendentals=2 * 10**6),
    )(
        latent, gn_gain.reshape(1, C), gn_bias.reshape(1, C), w_query, w_key, w_value, w_out,
        out_bias.reshape(1, C), context_frames, *consts,
    )


def solution(mesh):
    placed = (P("clip", "space", None), P(), P(), P(), P(), P(), P(), P(), P("clip", None))
    return jax.shard_map(
        local, mesh=mesh, in_specs=placed, out_specs=P("clip", "space", None), check_vma=False
    )
```

```python
import numpy as np

import jax
import jax.numpy as jnp
from jax import lax
from jax.experimental import pallas as pl
from jax.experimental.pallas import tpu as pltpu
from jax.sharding import PartitionSpec as P

C = 1280
HEAD_DIM = 64
GROUPS = 32
FRAMES = 16
EDGE = 4
EPS = 1e-06
ROWS = 48
HALF = 24
KEYS = 112
TILE = 256
TILES = C // TILE
MESH = pl.DeviceIdType.MESH
F32, BF16 = jnp.float32, jnp.bfloat16


def swap_matrix(outer, inner, blocks=1):
    n = outer * inner
    m = np.zeros((n, n), np.float32)
    for i in range(outer):
        for j in range(inner):
            m[j * outer + i, i * inner + j] = 1
    return m


def edge_merge():
    m = np.zeros((192, 192), np.float32)
    for side in range(2):
        for p in range(HALF):
            for f in range(EDGE):
                m[p * 8 + side * 4 + f, side * 96 + p * 4 + f] = 1
    return m


SWAP16 = swap_matrix(16, 16)
SWAP8 = swap_matrix(16, 8)
EDGE_OUT = swap_matrix(EDGE, ROWS)
EDGE_IN = edge_merge()
GROUP_OF = np.zeros((C, 128), np.float32)
GROUP_OF[np.arange(C), np.arange(C) // (C // GROUPS)] = 1
HEAD_MASK = np.zeros((128, TILE), np.float32)
for _h in range(4):
    HEAD_MASK[_h * 32 : _h * 32 + 32, _h * 64 : _h * 64 + 64] = 1


def dot(a, b):
    return jnp.dot(a, b, preferred_element_type=F32)


def exact_dot(a, b):
    return jnp.dot(a, b, preferred_element_type=F32, precision=lax.Precision.HIGHEST)


def slot_of(i, j, s):
    return j * 8 + i * 2 + s


def kernel(
    latent, gain, shift, wq, wk, wv, wo, out_bias, picks, swap16, swap8, edge_out, edge_in, group_of, group_to, head_mask,
    out,
    lat, normed, turned, sib, ctx, xc, edge_tx, edge_rx, edge_x, query, kv, att, att_tx, result, w, w_out,
    s16, s8, e_out, e_in, g_of, g_to, h_mask, stat_tx, stat_rx, pick_own, pick_tx, pick_rx, mask,
    load_sem, send_sem, recv_sem, misc_tx, misc_rx, att_sem_tx, att_sem_rx, store_sem,
):
    clip = lax.axis_index("clip")
    space = lax.axis_index("space")
    core = clip % 2
    y = (clip // 2) % 2
    z = (clip // 4) % 4
    x = clip // 16
    chip = clip // 2

    def device(x, z, y, core):
        return (((x * 4 + z) * 2 + y) * 2 + core, space)

    def along(first, step):
        on_x = (1 - core) if first else core
        return device((x + step * on_x) % 4, (z + step * (1 - on_x)) % 4, y, core)

    a_up, a_down = along(True, 1), along(True, 3)
    b_up, b_down = along(False, 1), along(False, 3)
    y_pair = device(x, z, 1 - y, core)
    sibling = (clip + 1 - 2 * core, space)
    other_space = (clip, 1 - space)
    edge_chip = (chip + 2 * core + 31) % 32
    edge_to = [(edge_chip * 2, space), (edge_chip * 2 + 1, space)]
    edge_from = [(((chip + 31) % 32) * 2 + 1, space), (((chip + 1) % 32) * 2, space)]

    barrier = pltpu.get_barrier_semaphore()
    greet = [a_up, a_down, b_up, b_down, y_pair, sibling, other_space] + edge_to + edge_from
    for other in greet:
        pl.semaphore_signal(barrier, inc=1, device_id=other, device_id_type=MESH)

    loads = [
        pltpu.make_async_copy(src, dst, load_sem.at[n])
        for n, (src, dst) in enumerate(
            [
                (latent, lat),
                (group_of, g_of),
                (group_to, g_to),
                (swap16, s16),
                (edge_out, e_out),
                (wq, w.at[0]),
                (wk, w.at[1]),
                (wv, w.at[2]),
                (swap8, s8),
                (edge_in, e_in),
                (head_mask, h_mask),
                (wo, w_out),
            ]
        )
    ]
    for copy in loads:
        copy.start()

    row = lax.broadcasted_iota(jnp.int32, (48, 128), 0)
    lane = lax.broadcasted_iota(jnp.int32, (48, 128), 1)
    q_clip = (((lane >> 4) & 1) + core) & 1
    k_clip = (((row >> 4) & 1) + core) & 1
    frame = row & 15
    local = (row < 32) & (
        (k_clip == q_clip)
        | ((q_clip == 0) & (frame < EDGE))
        | ((q_clip == 1) & (frame >= FRAMES - EDGE))
    )
    left = (row >= 32) & (row < 36) & (q_clip == 0) & (chip > 0)
    right = (row >= 36) & (row < 40) & (q_clip == 1) & (chip < 31)
    mask[...] = jnp.where(local | left | right, 0.0, -jnp.inf).astype(F32)

    loads[0].wait()

    def add_rows(f, acc):
        v = lat[f].astype(F32)
        for r in range(ROWS // 8):
            acc = acc + v[8 * r : 8 * r + 8]
        return acc

    total = lax.fori_loop(0, FRAMES, add_rows, jnp.zeros((8, C), F32))
    loads[1].wait()
    loads[2].wait()
    count = FRAMES * ROWS * (C // GROUPS)
    mean_here = jnp.sum(exact_dot(total, g_of[...]), axis=0, keepdims=True) * (1.0 / count)
    mean_here = jnp.broadcast_to(mean_here, (8, 128))
    wide = exact_dot(mean_here, g_to[...])

    def add_squares(f, acc):
        v = lat[f].astype(F32)
        for r in range(ROWS // 8):
            d = v[8 * r : 8 * r + 8] - wide
            acc = acc + d * d
        return acc

    squares = lax.fori_loop(0, FRAMES, add_squares, jnp.zeros((8, C), F32))
    dev_here = jnp.sum(exact_dot(squares, g_of[...]), axis=0, keepdims=True)
    dev_here = jnp.broadcast_to(dev_here, (8, 128))
    first_row = lax.broadcasted_iota(jnp.int32, (8, 128), 0) == 0
    stat_tx[...] = jnp.where(first_row, mean_here, dev_here)

    pl.semaphore_wait(barrier, len(greet))

    def misc(n, src, dst, to):
        return pltpu.make_async_remote_copy(
            src_ref=src, dst_ref=dst, send_sem=misc_tx.at[n], recv_sem=misc_rx.at[n], device_id=to, device_id_type=MESH
        )

    stats = misc(0, stat_tx, stat_rx, other_space)
    stats.start()
    stats.wait_recv()
    mean_there = stat_rx[0:1]
    dev_there = stat_rx[1:2]
    gap = mean_here[0:1] - mean_there
    mean = 0.5 * (mean_here[0:1] + mean_there)
    var = (dev_here[0:1] + dev_there + gap * gap * (0.5 * count)) * (0.5 / count)
    scale = lax.rsqrt(var + EPS)
    both = jnp.where(first_row, jnp.broadcast_to(mean, (8, 128)), jnp.broadcast_to(scale, (8, 128)))
    both = exact_dot(both, g_to[...])
    mean_c = both[0:1]
    gain_c = both[1:2] * gain[...].reshape(1, C)
    shift_c = shift[...].reshape(1, C)

    def norm(v):
        return ((v.astype(F32) - mean_c) * gain_c + shift_c).astype(BF16)

    picked = norm(lat[picks[0, 0]]).astype(F32)
    low, high = picked[:HALF], picked[HALF:]
    pick_own[...] = jnp.where(core == 0, low, high)
    pick_tx[...] = jnp.where(core == 0, high, low)
    swap_pick = misc(1, pick_tx, pick_rx, sibling)
    swap_pick.start()

    def normalize(f, _):
        normed[f] = norm(lat[f])
        return 0

    lax.fori_loop(0, FRAMES, normalize, 0)

    swap_pick.wait_recv()
    for g in range(3):
        pair = jnp.concatenate([pick_own[8 * g : 8 * g + 8], pick_rx[8 * g : 8 * g + 8]], axis=0)
        ctx[g, 0:16, :] = pair.astype(BF16)

    def hop(i, j, s):
        if j == 0:
            if i == 0:
                src, to = (0, 0, 0), y_pair
            elif i == 1:
                src, to = (0, 0, s), a_up
            elif i == 2:
                src, to = (0, 0, s), a_down
            else:
                src, to = ((1, 0, 0), a_up) if s == 0 else ((2, 0, 1), a_down)
        elif j == 1:
            src, to = (i, 0, s), b_up
        elif j == 2:
            src, to = (i, 0, s), b_down
        else:
            src, to = ((i, 1, 0), b_up) if s == 0 else ((i, 2, 1), b_down)
        n, dst = slot_of(*src), slot_of(i, j, s)
        return pltpu.make_async_remote_copy(
            src_ref=ctx.at[:, 16 * n : 16 * n + 16, :],
            dst_ref=ctx.at[:, 16 * dst : 16 * dst + 16, :],
            send_sem=send_sem.at[dst],
            recv_sem=recv_sem.at[dst],
            device_id=to,
            device_id_type=MESH,
        )

    def start(*slots):
        for slot in slots:
            hop(*slot).start()

    start((0, 0, 1), (1, 0, 0), (2, 0, 0), (0, 1, 0), (0, 2, 0))

    loads[3].wait()

    for q in range(3):
        rows = normed[:, 16 * q : 16 * q + 16, :].reshape(256, C)
        turned[16 * q : 16 * q + 16] = dot(s16[...], rows).astype(BF16).reshape(16, 16, C)
    swap_rows = misc(2, turned.at[pl.ds(HALF * (1 - core), HALF)], sib, sibling)
    swap_rows.start()
    loads[4].wait()
    edge_rows = normed[pl.ds(12 * core, EDGE)].reshape(EDGE * ROWS, C)
    edge_tx[...] = dot(e_out[...], edge_rows).astype(BF16).reshape(2, 96, C)
    edge_sends = [
        pltpu.make_async_remote_copy(
            src_ref=edge_tx.at[k],
            dst_ref=edge_rx.at[1 - core],
            send_sem=misc_tx.at[3 + k],
            recv_sem=misc_rx.at[3 + 1 - core],
            device_id=edge_to[k],
            device_id_type=MESH,
        )
        for k in range(2)
    ]
    for copy in edge_sends:
        copy.start()

    def edge_arrived(n):
        pltpu.make_async_copy(edge_rx.at[n], edge_rx.at[n], misc_rx.at[3 + n]).wait()

    def pass_on(arrived, *slots):
        def act():
            hop(*arrived).wait_recv()
            start(*slots)

        return act

    def forward(i, s):
        return pass_on((i, 1, 0), (i, 3, 0)) if s == 0 else pass_on((i, 2, 1), (i, 3, 1))

    def project(rows, m, dst, at, factor=None):
        res = dot(rows, w[m])
        if factor is not None:
            res = res * factor
        dst[:, at : at + 16, :] = res.astype(BF16).reshape(HALF, 16, C)

    def project_query(rows, at):
        project(rows, 0, query, at, HEAD_DIM**-0.5)

    def project_kv(rows, at, acts=()):
        def step(m, _):
            for n, act in enumerate(acts):
                pl.when(m == n)(act)
            project(rows(), 1 + m, kv.at[m], at)
            return 0

        lax.fori_loop(0, 2, step, 0)

    def own_rows():
        return turned[pl.ds(HALF * core, HALF)].reshape(HALF * 16, C)

    def sib_rows():
        return sib[...].reshape(HALF * 16, C)

    def ctx_rows():
        return xc[...]

    def gather_ctx(j):
        for g in range(3):
            rows = dot(s8[...], ctx[g, 128 * j : 128 * j + 128, :])
            xc[128 * g : 128 * g + 128] = rows.astype(BF16)

    def many(*acts):
        def act():
            for one in acts:
                one()

        return act

    loads[5].wait()
    project_query(own_rows(), 0)
    loads[6].wait()
    loads[7].wait()
    project_kv(
        own_rows, 64,
        [
            pass_on((0, 0, 1), (1, 0, 1), (2, 0, 1), (0, 1, 1), (0, 2, 1)),
            many(
                pass_on((1, 0, 0), (3, 0, 0), (1, 1, 0), (1, 2, 0)),
                pass_on((2, 0, 0), (2, 1, 0), (2, 2, 0)),
            ),
        ],
    )
    swap_rows.wait_recv()
    project_query(sib_rows(), 16)
    project_kv(
        sib_rows, 80,
        [
            many(
                pass_on((2, 0, 1), (3, 0, 1), (2, 1, 1), (2, 2, 1)),
                pass_on((1, 0, 1), (1, 1, 1), (1, 2, 1)),
            ),
            many(
                pass_on((3, 0, 0), (3, 1, 0), (3, 2, 0)),
                forward(0, 0),
            ),
        ],
    )
    pass_on((3, 0, 1), (3, 1, 1), (3, 2, 1))()
    forward(0, 1)()
    loads[8].wait()
    gather_ctx(0)
    project_kv(ctx_rows, 0, [forward(1, 0), many(forward(2, 0), forward(2, 1))])

    loads[9].wait()
    edge_arrived(0)
    edge_arrived(1)
    edge_x[...] = dot(e_in[...], edge_rx[...].reshape(192, C)).astype(BF16)

    def edge_step(m, _):
        pl.when(m == 0)(forward(1, 1))
        pl.when(m == 1)(many(forward(3, 0), forward(3, 1)))
        res = dot(edge_x[...], w[1 + m]).reshape(HALF, 8, C)
        res = jnp.concatenate([res, jnp.zeros((HALF, 8, C), F32)], axis=1)
        kv[m, :, 96:112, :] = res.astype(BF16)
        return 0

    lax.fori_loop(0, 2, edge_step, 0)

    for i in range(4):
        hop(i, 1, 1).wait_recv()
    gather_ctx(1)
    project_kv(ctx_rows, 16)
    for i in range(4):
        hop(i, 2, 0).wait_recv()
    gather_ctx(2)
    project_kv(ctx_rows, 32)
    for i in range(4):
        for s in range(2):
            hop(i, 3, s).wait_recv()
    gather_ctx(3)
    project_kv(ctx_rows, 48)

    loads[10].wait()
    loads[11].wait()

    def send_att(c):
        there = pl.ds(HALF * core + 8 * c, 8)
        return pltpu.make_async_remote_copy(
            src_ref=att_tx.at[8 * c : 8 * c + 8],
            dst_ref=att.at[there],
            send_sem=att_sem_tx.at[c],
            recv_sem=att_sem_rx.at[c],
            device_id=sibling,
            device_id_type=MESH,
        )

    def attend(block, _):
        half = lax.broadcasted_iota(jnp.int32, (32, 128), 1) < HEAD_DIM
        units = [(block * 4 + n, h) for n in range(4) for h in range(TILES)]
        cols = [slice(h * TILE, (h + 1) * TILE) for h in range(TILES)]
        scores, weights, mixed = [], [], []
        for p, h in units:
            q = jnp.concatenate([query[p, :, cols[h]]] * 4, axis=0) * h_mask[...]
            scores.append(
                lax.dot_general(kv[0, p, :, cols[h]], q, (((1,), (1,)), ((), ())), preferred_element_type=F32)
            )
        for s in scores:
            s = jnp.concatenate([s[:64], s[64:] + mask[...]], axis=0)
            expo = jnp.exp(s - jnp.max(s, axis=0, keepdims=True))
            share = 1.0 / jnp.sum(expo, axis=0, keepdims=True)
            weights.append((expo * share).astype(BF16))
        for (p, h), s in zip(units, weights):
            mixed.append(
                lax.dot_general(s, kv[1, p, :, cols[h]], (((0,), (0,)), ((), ())), preferred_element_type=F32)
            )
        for (p, h), m in zip(units, mixed):
            for t in range(2):
                lanes = slice(128 * t, 128 * t + 128)
                both = jnp.where(half, m[64 * t : 64 * t + 32, lanes], m[64 * t + 32 : 64 * t + 64, lanes])
                both = both.astype(BF16)
                to = slice(h * TILE + 128 * t, h * TILE + 128 * t + 128)
                att[HALF * core + p, :, to] = both[:16]
                att_tx[p, :, to] = both[16:]
        return 0

    for c in range(3):
        lax.fori_loop(2 * c, 2 * c + 2, attend, 0)
        send_att(c).start()
    for c in range(3):
        there = pl.ds(HALF * (1 - core) + 8 * c, 8)
        pltpu.make_async_copy(att.at[there], att.at[there], att_sem_rx.at[c]).wait()

    for q in range(3):
        rows = dot(s16[...], att[16 * q : 16 * q + 16].reshape(256, C))
        normed[:, 16 * q : 16 * q + 16, :] = rows.astype(BF16).reshape(16, 16, C)
    res = dot(normed[...].reshape(FRAMES * ROWS, C), w_out[...])
    res = lat[...].astype(F32) + res.reshape(FRAMES, ROWS, C) + out_bias[...].reshape(1, 1, C)
    result[...] = res.astype(BF16)
    store = pltpu.make_async_copy(result, out, store_sem)
    store.start()

    stats.wait_send()
    swap_pick.wait_send()
    swap_rows.wait_send()
    for copy in edge_sends:
        copy.wait_send()
    for j in range(4):
        for i in range(4):
            for s in range(2):
                if (i, j, s) != (0, 0, 0):
                    hop(i, j, s).wait_send()
    for c in range(3):
        send_att(c).wait_send()
    store.wait()


def local(latent, gn_gain, gn_bias, w_query, w_key, w_value, w_out, out_bias, context_frames):
    consts = [
        jnp.asarray(SWAP16, BF16),
        jnp.asarray(SWAP8, BF16),
        jnp.asarray(EDGE_OUT, BF16),
        jnp.asarray(EDGE_IN, BF16),
        jnp.asarray(GROUP_OF, F32),
        jnp.asarray(GROUP_OF.T.copy(), F32),
        jnp.asarray(HEAD_MASK, BF16),
    ]
    any_ = pl.BlockSpec(memory_space=pl.ANY)
    vmem = pl.BlockSpec(memory_space=pltpu.VMEM)
    smem = pl.BlockSpec(memory_space=pltpu.SMEM)
    dma = pltpu.SemaphoreType.DMA
    return pl.pallas_call(
        kernel,
        out_shape=jax.ShapeDtypeStruct((FRAMES, ROWS, C), BF16),
        in_specs=[any_, vmem, vmem, any_, any_, any_, any_, vmem, smem] + [any_] * 7,
        out_specs=any_,
        scratch_shapes=[
            pltpu.VMEM((FRAMES, ROWS, C), BF16),
            pltpu.VMEM((FRAMES, ROWS, C), BF16),
            pltpu.VMEM((ROWS, FRAMES, C), BF16),
            pltpu.VMEM((HALF, FRAMES, C), BF16),
            pltpu.VMEM((3, 512, C), BF16),
            pltpu.VMEM((HALF * 16, C), BF16),
            pltpu.VMEM((2, 96, C), BF16),
            pltpu.VMEM((2, 96, C), BF16),
            pltpu.VMEM((192, C), BF16),
            pltpu.VMEM((HALF, 32, C), BF16),
            pltpu.VMEM((2, HALF, KEYS, C), BF16),
            pltpu.VMEM((ROWS, FRAMES, C), BF16),
            pltpu.VMEM((HALF, FRAMES, C), BF16),
            pltpu.VMEM((FRAMES, ROWS, C), BF16),
            pltpu.VMEM((3, C, C), BF16),
            pltpu.VMEM((C, C), BF16),
            pltpu.VMEM((256, 256), BF16),
            pltpu.VMEM((128, 128), BF16),
            pltpu.VMEM((192, 192), BF16),
            pltpu.VMEM((192, 192), BF16),
            pltpu.VMEM((C, 128), F32),
            pltpu.VMEM((128, C), F32),
            pltpu.VMEM((128, TILE), BF16),
            pltpu.VMEM((8, 128), F32),
            pltpu.VMEM((8, 128), F32),
            pltpu.VMEM((HALF, C), F32),
            pltpu.VMEM((HALF, C), F32),
            pltpu.VMEM((HALF, C), F32),
            pltpu.VMEM((48, 128), F32),
            dma((12,)),
            dma((32,)),
            dma((32,)),
            dma((5,)),
            dma((5,)),
            dma((3,)),
            dma((3,)),
            dma,
        ],
        compiler_params=pltpu.CompilerParams(
            collective_id=0, has_side_effects=True, vmem_limit_bytes=60 * 1024 * 1024
        ),
        cost_estimate=pl.CostEstimate(flops=25 * 10**9, bytes_accessed=18 * 10**6, transcendentals=2 * 10**6),
    )(
        latent, gn_gain, gn_bias, w_query, w_key, w_value, w_out,
        out_bias, context_frames, *consts,
    )


def solution(mesh):
    placed = (P("clip", "space", None), P(), P(), P(), P(), P(), P(), P(), P("clip", None))
    return jax.shard_map(
        local, mesh=mesh, in_specs=placed, out_specs=P("clip", "space", None), check_vma=False
    )
```

```python
import numpy as np

import jax
import jax.numpy as jnp
from jax import lax
from jax.experimental import pallas as pl
from jax.experimental.pallas import tpu as pltpu
from jax.sharding import PartitionSpec as P

C = 1280
HEAD_DIM = 64
GROUPS = 32
FRAMES = 16
EDGE = 4
EPS = 1e-06
ROWS = 48
HALF = 24
KEYS = 112
TILE = 256
TILES = C // TILE
MESH = pl.DeviceIdType.MESH
F32, BF16 = jnp.float32, jnp.bfloat16


def swap_matrix(outer, inner, blocks=1):
    n = outer * inner
    m = np.zeros((n, n), np.float32)
    for i in range(outer):
        for j in range(inner):
            m[j * outer + i, i * inner + j] = 1
    return m


def edge_merge():
    m = np.zeros((192, 192), np.float32)
    for side in range(2):
        for p in range(HALF):
            for f in range(EDGE):
                m[p * 8 + side * 4 + f, side * 96 + p * 4 + f] = 1
    return m


SWAP16 = swap_matrix(16, 16)
SWAP8 = swap_matrix(16, 8)
EDGE_OUT = swap_matrix(EDGE, ROWS)
EDGE_IN = edge_merge()
GROUP_OF = np.zeros((C, 128), np.float32)
GROUP_OF[np.arange(C), np.arange(C) // (C // GROUPS)] = 1
HEAD_MASK = np.zeros((128, TILE), np.float32)
for _h in range(4):
    HEAD_MASK[_h * 32 : _h * 32 + 32, _h * 64 : _h * 64 + 64] = 1


def dot(a, b):
    return jnp.dot(a, b, preferred_element_type=F32)


def exact_dot(a, b):
    high = a.astype(BF16).astype(F32)
    mid = (a - high).astype(BF16).astype(F32)
    low = a - high - mid
    n = a.shape[0]
    res = dot(jnp.concatenate([high, mid, low], axis=0).astype(BF16), b)
    return res[:n] + res[n : 2 * n] + res[2 * n :]


def slot_of(i, j, s):
    return j * 8 + i * 2 + s


def kernel(
    latent, gain_in, shift_in, wq, wk, wv, wo, bias_in, picks, swap16, swap8, edge_out, edge_in, group_of, group_to, head_mask,
    out,
    lat, turned, sib, own_x, ctx, xc, edge_tx, edge_relay, edge_rx, edge_x, query, kv, att, att_tx, result, w, w_out,
    s16, s8, e_out, e_in, g_of, g_to, h_mask, gain, shift, out_bias, stat_tx, stat_rx, final_tx, final_rx, pick_own, pick_tx, pick_rx, mask,
    load_sem, send_sem, recv_sem, misc_tx, misc_rx, stat_sem_tx, stat_sem_rx, final_sem_tx, final_sem_rx, relay_rx, att_sem_tx, att_sem_rx, store_sem,
):
    clip = lax.axis_index("clip")
    space = lax.axis_index("space")
    core = clip % 2
    y = (clip // 2) % 2
    z = (clip // 4) % 4
    x = clip // 16
    chip = clip // 2

    def device(x, z, y, core):
        return (((x * 4 + z) * 2 + y) * 2 + core, space)

    def along(first, step):
        on_x = (1 - core) if first else core
        return device((x + step * on_x) % 4, (z + step * (1 - on_x)) % 4, y, core)

    a_up, a_down = along(True, 1), along(True, 3)
    b_up, b_down = along(False, 1), along(False, 3)
    y_pair = device(x, z, 1 - y, core)
    sibling = (clip + 1 - 2 * core, space)
    stats_to = [(clip, 1 - space), sibling, (clip + 1 - 2 * core, 1 - space)]
    edge_chip = (chip + 2 * core + 31) % 32
    edge_to = [(edge_chip * 2, space), (edge_chip * 2 + 1, space)]
    edge_from = [(((chip + 31) % 32) * 2 + 1, space), (((chip + 1) % 32) * 2, space)]

    relay_z = (z + 2 * y + 3) % 4
    relay_to = [device(x, relay_z, y, k) for k in range(2)]
    origin_z = (z + 5 - 2 * y) % 4
    relay_from = [device(x, origin_z, y, k) for k in range(2)]
    pass_chip = ((x * 4 + origin_z) * 2 + y + 2 * y + 31) % 32
    pass_to = (pass_chip * 2 + core, space)
    near = (chip + 2 * y + 31) % 32
    pass_from = device(near // 8, ((near // 2) % 4 + 2 * (1 - y) + 3) % 4, 1 - y, core)

    edge_up = core * y * (1 - (z + 2) // 3)
    edge_down = core * (1 - y) * (z // 3)

    barrier = pltpu.get_barrier_semaphore()
    greet = [a_up, a_down, b_up, b_down, y_pair] + stats_to + edge_to + edge_from
    greet += relay_to + relay_from + [pass_to, pass_from]
    for other in greet:
        pl.semaphore_signal(barrier, inc=1, device_id=other, device_id_type=MESH)

    loads = [
        pltpu.make_async_copy(src, dst, load_sem.at[n])
        for n, (src, dst) in enumerate(
            [
                (latent, lat),
                (group_of, g_of),
                (group_to, g_to),
                (swap16, s16),
                (edge_out, e_out),
                (gain_in, gain),
                (shift_in, shift),
                (bias_in, out_bias),
                (wq, w.at[0]),
                (wk, w.at[1]),
                (wv, w.at[2]),
                (swap8, s8),
                (edge_in, e_in),
                (head_mask, h_mask),
                (wo, w_out),
            ]
        )
    ]
    for copy in loads[:8]:
        copy.start()

    row = lax.broadcasted_iota(jnp.int32, (48, 128), 0)
    lane = lax.broadcasted_iota(jnp.int32, (48, 128), 1)
    q_clip = (((lane >> 4) & 1) + core) & 1
    k_clip = (((row >> 4) & 1) + core) & 1
    frame = row & 15
    local = (row < 32) & (
        (k_clip == q_clip)
        | ((q_clip == 0) & (frame < EDGE))
        | ((q_clip == 1) & (frame >= FRAMES - EDGE))
    )
    left = (row >= 32) & (row < 36) & (q_clip == 0) & (chip > 0)
    right = (row >= 36) & (row < 40) & (q_clip == 1) & (chip < 31)
    mask[...] = jnp.where(local | left | right, 0.0, -jnp.inf).astype(F32)

    loads[0].wait()
    for copy in loads[8:]:
        copy.start()

    def add_rows(f, acc):
        v = lat[f].astype(F32)
        for r in range(ROWS // 8):
            acc = acc + v[8 * r : 8 * r + 8]
        return acc

    total = lax.fori_loop(0, FRAMES, add_rows, jnp.zeros((8, C), F32))
    loads[1].wait()
    loads[2].wait()
    count = FRAMES * ROWS * (C // GROUPS)
    mean_here = jnp.sum(exact_dot(total, g_of[...]), axis=0, keepdims=True) * (1.0 / count)
    mean_here = jnp.broadcast_to(mean_here, (8, 128))
    wide = exact_dot(mean_here, g_to[...])

    def add_squares(f, acc):
        v = lat[f].astype(F32)
        for r in range(ROWS // 8):
            d = v[8 * r : 8 * r + 8] - wide
            acc = acc + d * d
        return acc

    squares = lax.fori_loop(0, FRAMES, add_squares, jnp.zeros((8, C), F32))
    dev_here = jnp.sum(exact_dot(squares, g_of[...]), axis=0, keepdims=True)
    dev_here = jnp.broadcast_to(dev_here, (8, 128))
    first_row = lax.broadcasted_iota(jnp.int32, (8, 128), 0) == 0
    stat_tx[...] = jnp.where(first_row, mean_here, dev_here)

    picked = lat[picks[0, 0]].astype(F32)
    low, high = picked[:HALF], picked[HALF:]
    pick_own[...] = jnp.where(core == 0, low, high)
    pick_tx[...] = jnp.where(core == 0, high, low)

    pl.semaphore_wait(barrier, len(greet))

    def misc(n, src, dst, to):
        return pltpu.make_async_remote_copy(
            src_ref=src, dst_ref=dst, send_sem=misc_tx.at[n], recv_sem=misc_rx.at[n], device_id=to, device_id_type=MESH
        )

    stats = [
        pltpu.make_async_remote_copy(
            src_ref=stat_tx,
            dst_ref=stat_rx.at[n],
            send_sem=stat_sem_tx.at[n],
            recv_sem=stat_sem_rx.at[n],
            device_id=to,
            device_id_type=MESH,
        )
        for n, to in enumerate(stats_to)
    ]
    for copy in stats:
        copy.start()
    swap_pick = misc(1, pick_tx, pick_rx, sibling)
    swap_pick.start()

    loads[4].wait()
    edge_rows = lat[pl.ds(12 * core, EDGE)].reshape(EDGE * ROWS, C)
    edge_tx[...] = dot(e_out[...], edge_rows).astype(BF16).reshape(2, 96, C)
    relays = [
        pltpu.make_async_remote_copy(
            src_ref=edge_tx.at[k],
            dst_ref=edge_relay,
            send_sem=misc_tx.at[3 + k],
            recv_sem=relay_rx,
            device_id=relay_to[k],
            device_id_type=MESH,
        )
        for k in range(2)
    ]
    directs = [
        pltpu.make_async_remote_copy(
            src_ref=edge_tx.at[k],
            dst_ref=edge_rx.at[1 - core],
            send_sem=misc_tx.at[5 + k],
            recv_sem=misc_rx.at[3 + 1 - core],
            device_id=edge_to[k],
            device_id_type=MESH,
        )
        for k in range(2)
    ]
    passing = pltpu.make_async_remote_copy(
        src_ref=edge_relay,
        dst_ref=edge_rx.at[1 - y],
        send_sem=misc_tx.at[7],
        recv_sem=misc_rx.at[3 + 1 - y],
        device_id=pass_to,
        device_id_type=MESH,
    )

    @pl.when(core == y)
    def _():
        for copy in relays:
            copy.start()

    def send_edges():
        @pl.when(core != y)
        def _():
            for copy in directs:
                copy.start()

        relays[0].wait_recv()
        passing.start()

    loads[3].wait()
    for q in range(3):
        rows = lat[:, 16 * q : 16 * q + 16, :].reshape(256, C)
        turned[16 * q : 16 * q + 16] = dot(s16[...], rows).astype(BF16).reshape(16, 16, C)
    swap_rows = misc(2, turned.at[pl.ds(HALF * (1 - core), HALF)], sib, sibling)
    swap_rows.start()

    for copy in stats:
        copy.wait_recv()

    loads[5].wait()
    loads[6].wait()

    def combine(one, two):
        mean_one, mean_two = one[0:1], two[0:1]
        gap = mean_one - mean_two
        var = (one[1:2] + two[1:2] + gap * gap * (0.5 * count)) * (0.5 / count)
        return [0.5 * (mean_one + mean_two), lax.rsqrt(var + EPS)]

    table = combine(stat_tx[...], stat_rx[0]) + combine(stat_rx[1], stat_rx[2])
    final_tx[...] = jnp.concatenate(table + table, axis=0)
    final_sends = [
        pltpu.make_async_remote_copy(
            src_ref=final_tx,
            dst_ref=final_rx.at[1 - core],
            send_sem=final_sem_tx.at[k],
            recv_sem=final_sem_rx.at[1 - core],
            device_id=edge_to[k],
            device_id_type=MESH,
        )
        for k in range(2)
    ]
    for copy in final_sends:
        copy.start()
    table = exact_dot(final_tx[...], g_to[...])
    gains = gain[...].reshape(1, C)
    shifts = shift[...].reshape(1, C)

    def norm(v, sib_clip):
        at = 2 if sib_clip else 0
        return (v.astype(F32) - table[at : at + 1]) * (table[at + 1 : at + 2] * gains) + shifts

    swap_pick.wait_recv()
    for g in range(3):
        part = slice(8 * g, 8 * g + 8)
        pair = jnp.concatenate([norm(pick_own[part], False), norm(pick_rx[part], True)], axis=0)
        ctx[g, 0:16, :] = pair.astype(BF16)

    def leaves_down(i, s):
        if i < 2:
            return edge_up if s == 0 else 1 - edge_down
        return s

    def hop(i, j, s):
        if j == 0:
            if i == 0:
                src, to = (0, 0, 0), y_pair
            elif i == 1:
                src, to = (0, 0, s), a_up
            elif i == 2:
                src, to = (0, 0, s), a_down
            else:
                src, to = ((1, 0, 0), a_up) if s == 0 else ((2, 0, 1), a_down)
        elif j == 1:
            src, to = (i, 0, s), b_up
        elif j == 2:
            src, to = (i, 0, s), b_down
        else:
            down = leaves_down(i, s)
            src, to = (i, 1 + down, s), along(False, 1 + 2 * down)
        n, dst = slot_of(*src), slot_of(i, j, s)
        return pltpu.make_async_remote_copy(
            src_ref=ctx.at[:, pl.ds(pl.multiple_of(16 * n, 16), 16), :],
            dst_ref=ctx.at[:, 16 * dst : 16 * dst + 16, :],
            send_sem=send_sem.at[dst],
            recv_sem=recv_sem.at[dst],
            device_id=to,
            device_id_type=MESH,
        )

    def start(*slots):
        for slot in slots:
            hop(*slot).start()

    start((0, 0, 1), (1, 0, 0), (2, 0, 0), (0, 1, 0), (0, 2, 0))

    def edge_arrived(n):
        pltpu.make_async_copy(edge_rx.at[n], edge_rx.at[n], misc_rx.at[3 + n]).wait()
        pltpu.make_async_copy(final_rx.at[n], final_rx.at[n], final_sem_rx.at[n]).wait()

    def pass_on(arrived, *slots):
        def act():
            hop(*arrived).wait_recv()
            start(*slots)

        return act

    def arrive(i, j, s):
        n = slot_of(i, j, s)
        here = ctx.at[:, pl.ds(pl.multiple_of(16 * n, 16), 16), :]
        pltpu.make_async_copy(here, here, recv_sem.at[n]).wait()

    def forward(i, s):
        def act():
            arrive(i, 1 + leaves_down(i, s), s)
            start((i, 3, s))

        return act

    def project(rows, m):
        return dot(rows, w[m])

    def kv_steps(rows, store, *acts):
        def step(m, _):
            for n, act in enumerate(acts):
                pl.when(m == n)(act)
            store(m, project(rows(), 1 + m))
            return 0

        lax.fori_loop(0, 2, step, 0)

    def store_rows(at, n):
        def store(m, res):
            kv[m, :, at : at + n, :] = res.astype(BF16).reshape(HALF, n, C)

        return store

    def gather_ctx(j, at):
        for g in range(3):
            rows = dot(s8[...], ctx[g, 128 * j : 128 * j + 128, :]).astype(BF16)
            xc[8 * g : 8 * g + 8, at : at + 16, :] = rows.reshape(8, 16, C)

    def many(*acts):
        def act():
            for one in acts:
                one()

        return act

    own_x[:, 0:16, :] = norm(turned[pl.ds(HALF * core, HALF)], False).astype(BF16)
    swap_rows.wait_recv()
    own_x[:, 16:32, :] = norm(sib[...], True).astype(BF16)

    def own_rows():
        return own_x[...].reshape(HALF * 32, C)

    loads[8].wait()
    query[...] = (project(own_rows(), 0) * (HEAD_DIM**-0.5)).astype(BF16).reshape(HALF, 32, C)
    loads[9].wait()
    loads[10].wait()
    kv_steps(
        own_rows,
        store_rows(64, 32),
        many(
            pass_on((0, 0, 1), (1, 0, 1), (2, 0, 1), (0, 1, 1), (0, 2, 1)),
            pass_on((1, 0, 0), (3, 0, 0), (1, 1, 0), (1, 2, 0)),
            pass_on((2, 0, 0), (2, 1, 0), (2, 2, 0)),
            send_edges,
            forward(0, 0),
        ),
        many(
            pass_on((2, 0, 1), (3, 0, 1), (2, 1, 1), (2, 2, 1)),
            pass_on((1, 0, 1), (1, 1, 1), (1, 2, 1)),
        ),
    )
    pass_on((3, 0, 0), (3, 1, 0), (3, 2, 0))()
    forward(0, 1)()
    pass_on((3, 0, 1), (3, 1, 1), (3, 2, 1))()
    loads[11].wait()
    gather_ctx(0, 0)

    def one_phase():
        return xc[:, 0:16, :].reshape(HALF * 16, C)

    kv_steps(one_phase, store_rows(0, 16), forward(1, 0), many(forward(2, 0), forward(2, 1)))

    forward(1, 1)()
    forward(3, 0)()
    forward(3, 1)()
    for i in range(4):
        for s in range(2):
            arrive(i, 2 - leaves_down(i, s), s)
    gather_ctx(1, 0)
    gather_ctx(2, 16)
    kv_steps(lambda: xc[...].reshape(HALF * 32, C), store_rows(16, 32))
    loads[12].wait()
    edge_arrived(0)
    edge_arrived(1)
    left_side = lax.broadcasted_iota(jnp.int32, (8, C), 0) < EDGE
    left_table = exact_dot(final_rx[0], g_to[...])
    right_table = exact_dot(final_rx[1], g_to[...])
    edge_mean = jnp.where(left_side, left_table[0:1], right_table[0:1])
    edge_gain = jnp.where(left_side, left_table[1:2] * gains, right_table[1:2] * gains)
    rows = dot(e_in[...], edge_rx[...].reshape(192, C)).reshape(HALF, 8, C)
    edge_x[...] = ((rows - edge_mean) * edge_gain + shifts).astype(BF16).reshape(HALF * 8, C)

    def edge_rows_in():
        return edge_x[...]

    def store_edges(m, res):
        res = jnp.concatenate([res.reshape(HALF, 8, C), jnp.zeros((HALF, 8, C), F32)], axis=1)
        kv[m, :, 96:112, :] = res.astype(BF16)

    kv_steps(edge_rows_in, store_edges)

    for i in range(4):
        for s in range(2):
            hop(i, 3, s).wait_recv()
    gather_ctx(3, 0)
    kv_steps(one_phase, store_rows(48, 16))

    loads[13].wait()
    loads[14].wait()

    def send_att(c):
        there = pl.ds(HALF * core + 8 * c, 8)
        return pltpu.make_async_remote_copy(
            src_ref=att_tx.at[8 * c : 8 * c + 8],
            dst_ref=att.at[there],
            send_sem=att_sem_tx.at[c],
            recv_sem=att_sem_rx.at[c],
            device_id=sibling,
            device_id_type=MESH,
        )

    def attend(block, _):
        half = lax.broadcasted_iota(jnp.int32, (32, 128), 1) < HEAD_DIM
        units = [(block * 4 + n, h) for n in range(4) for h in range(TILES)]
        cols = [slice(h * TILE, (h + 1) * TILE) for h in range(TILES)]
        scores, weights, mixed = [], [], []
        for p, h in units:
            q = jnp.concatenate([query[p, :, cols[h]]] * 4, axis=0) * h_mask[...]
            scores.append(
                lax.dot_general(kv[0, p, :, cols[h]], q, (((1,), (1,)), ((), ())), preferred_element_type=F32)
            )
        for s in scores:
            s = jnp.concatenate([s[:64], s[64:] + mask[...]], axis=0)
            expo = jnp.exp(s - jnp.max(s, axis=0, keepdims=True))
            share = 1.0 / jnp.sum(expo, axis=0, keepdims=True)
            weights.append((expo * share).astype(BF16))
        for (p, h), s in zip(units, weights):
            mixed.append(
                lax.dot_general(s, kv[1, p, :, cols[h]], (((0,), (0,)), ((), ())), preferred_element_type=F32)
            )
        for (p, h), m in zip(units, mixed):
            for t in range(2):
                lanes = slice(128 * t, 128 * t + 128)
                both = jnp.where(half, m[64 * t : 64 * t + 32, lanes], m[64 * t + 32 : 64 * t + 64, lanes])
                both = both.astype(BF16)
                to = slice(h * TILE + 128 * t, h * TILE + 128 * t + 128)
                att[HALF * core + p, :, to] = both[:16]
                att_tx[p, :, to] = both[16:]
        return 0

    for c in range(3):
        lax.fori_loop(2 * c, 2 * c + 2, attend, 0)
        send_att(c).start()

    def att_arrived(c):
        there = pl.ds(HALF * (1 - core) + 8 * c, 8)
        pltpu.make_async_copy(att.at[there], att.at[there], att_sem_rx.at[c]).wait()

    loads[7].wait()

    stores = []
    for t in range(3):
        if t == 1:
            att_arrived(0)
            att_arrived(1)
        elif t == 2:
            att_arrived(2)
        q = (t + 2 * core) % 3
        there = pl.ds(pl.multiple_of(q * 16, 16), 16)
        rows = dot(s16[...], att[there].reshape(256, C)).astype(BF16)
        res = dot(rows, w_out[...]).reshape(FRAMES, 16, C) + out_bias[...].reshape(1, 1, C)
        result[t] = (lat[:, there, :].astype(F32) + res).astype(BF16)
        stores.append(pltpu.make_async_copy(result.at[t], out.at[:, there, :], store_sem.at[t]))
        stores[t].start()

    for copy in stats:
        copy.wait_send()
    swap_pick.wait_send()
    swap_rows.wait_send()
    for copy in final_sends + [passing]:
        copy.wait_send()

    @pl.when(core == y)
    def _():
        for copy in relays:
            copy.wait_send()

    @pl.when(core != y)
    def _():
        for copy in directs:
            copy.wait_send()

    for j in range(4):
        for i in range(4):
            for s in range(2):
                if (i, j, s) != (0, 0, 0):
                    hop(i, j, s).wait_send()
    for c in range(3):
        send_att(c).wait_send()
    for copy in stores:
        copy.wait()


def local(latent, gn_gain, gn_bias, w_query, w_key, w_value, w_out, out_bias, context_frames):
    consts = [
        jnp.asarray(SWAP16, BF16),
        jnp.asarray(SWAP8, BF16),
        jnp.asarray(EDGE_OUT, BF16),
        jnp.asarray(EDGE_IN, BF16),
        jnp.asarray(GROUP_OF, BF16),
        jnp.asarray(GROUP_OF.T.copy(), BF16),
        jnp.asarray(HEAD_MASK, BF16),
    ]
    any_ = pl.BlockSpec(memory_space=pl.ANY)
    smem = pl.BlockSpec(memory_space=pltpu.SMEM)
    dma = pltpu.SemaphoreType.DMA
    return pl.pallas_call(
        kernel,
        out_shape=jax.ShapeDtypeStruct((FRAMES, ROWS, C), BF16),
        in_specs=[any_] * 8 + [smem] + [any_] * 7,
        out_specs=any_,
        scratch_shapes=[
            pltpu.VMEM((FRAMES, ROWS, C), BF16),
            pltpu.VMEM((ROWS, FRAMES, C), BF16),
            pltpu.VMEM((HALF, FRAMES, C), BF16),
            pltpu.VMEM((HALF, 32, C), BF16),
            pltpu.VMEM((3, 512, C), BF16),
            pltpu.VMEM((HALF, 32, C), BF16),
            pltpu.VMEM((2, 96, C), BF16),
            pltpu.VMEM((96, C), BF16),
            pltpu.VMEM((2, 96, C), BF16),
            pltpu.VMEM((192, C), BF16),
            pltpu.VMEM((HALF, 32, C), BF16),
            pltpu.VMEM((2, HALF, KEYS, C), BF16),
            pltpu.VMEM((ROWS, FRAMES, C), BF16),
            pltpu.VMEM((HALF, FRAMES, C), BF16),
            pltpu.VMEM((3, FRAMES, 16, C), BF16),
            pltpu.VMEM((3, C, C), BF16),
            pltpu.VMEM((C, C), BF16),
            pltpu.VMEM((256, 256), BF16),
            pltpu.VMEM((128, 128), BF16),
            pltpu.VMEM((192, 192), BF16),
            pltpu.VMEM((192, 192), BF16),
            pltpu.VMEM((C, 128), BF16),
            pltpu.VMEM((128, C), BF16),
            pltpu.VMEM((128, TILE), BF16),
            pltpu.VMEM((C,), F32),
            pltpu.VMEM((C,), F32),
            pltpu.VMEM((C,), F32),
            pltpu.VMEM((8, 128), F32),
            pltpu.VMEM((3, 8, 128), F32),
            pltpu.VMEM((8, 128), F32),
            pltpu.VMEM((2, 8, 128), F32),
            pltpu.VMEM((HALF, C), F32),
            pltpu.VMEM((HALF, C), F32),
            pltpu.VMEM((HALF, C), F32),
            pltpu.VMEM((48, 128), F32),
            dma((15,)),
            dma((32,)),
            dma((32,)),
            dma((8,)),
            dma((5,)),
            dma((3,)),
            dma((3,)),
            dma((2,)),
            dma((2,)),
            dma,
            dma((3,)),
            dma((3,)),
            dma((3,)),
        ],
        compiler_params=pltpu.CompilerParams(
            collective_id=0, has_side_effects=True, vmem_limit_bytes=60 * 1024 * 1024
        ),
        cost_estimate=pl.CostEstimate(flops=25 * 10**9, bytes_accessed=18 * 10**6, transcendentals=2 * 10**6),
    )(
        latent, gn_gain, gn_bias, w_query, w_key, w_value, w_out,
        out_bias, context_frames, *consts,
    )


def solution(mesh):
    placed = (P("clip", "space", None), P(), P(), P(), P(), P(), P(), P(), P("clip", None))
    return jax.shard_map(
        local, mesh=mesh, in_specs=placed, out_specs=P("clip", "space", None), check_vma=False
    )
```

```python
import numpy as np

import jax
import jax.numpy as jnp
from jax import lax
from jax.experimental import pallas as pl
from jax.experimental.pallas import tpu as pltpu
from jax.sharding import PartitionSpec as P

C = 1280
HEAD_DIM = 64
GROUPS = 32
FRAMES = 16
EDGE = 4
EPS = 1e-06
ROWS = 48
HALF = 24
KEYS = 112
TILE = 256
TILES = C // TILE
MESH = pl.DeviceIdType.MESH
F32, BF16 = jnp.float32, jnp.bfloat16


def swap_matrix(outer, inner, blocks=1):
    n = outer * inner
    m = np.zeros((n, n), np.float32)
    for i in range(outer):
        for j in range(inner):
            m[j * outer + i, i * inner + j] = 1
    return m


def edge_merge():
    m = np.zeros((192, 192), np.float32)
    for side in range(2):
        for p in range(HALF):
            for f in range(EDGE):
                m[p * 8 + side * 4 + f, side * 96 + p * 4 + f] = 1
    return m


SWAP16 = swap_matrix(16, 16)
SWAP8 = swap_matrix(16, 8)
EDGE_OUT = swap_matrix(EDGE, ROWS)
EDGE_IN = edge_merge()
GROUP_OF = np.zeros((C, 128), np.float32)
GROUP_OF[np.arange(C), np.arange(C) // (C // GROUPS)] = 1
HEAD_MASK = np.zeros((128, TILE), np.float32)
for _h in range(4):
    HEAD_MASK[_h * 32 : _h * 32 + 32, _h * 64 : _h * 64 + 64] = 1


def dot(a, b):
    return jnp.dot(a, b, preferred_element_type=F32)


def exact_dot(a, b):
    high = a.astype(BF16).astype(F32)
    mid = (a - high).astype(BF16).astype(F32)
    low = a - high - mid
    n = a.shape[0]
    res = dot(jnp.concatenate([high, mid, low], axis=0).astype(BF16), b)
    return res[:n] + res[n : 2 * n] + res[2 * n :]


def slot_of(i, j, s):
    return j * 8 + i * 2 + s


def kernel(
    latent, gain_in, shift_in, wq, wk, wv, wo, bias_in, picks, swap16, swap8, edge_out, edge_in, group_of, group_to, head_mask,
    out,
    lat, turned, sib, own_x, ctx, xc, edge_tx, edge_relay, edge_cross, edge_rx, edge_x, query, kv, att, att_tx, result, w, w_out,
    s16, s8, e_out, e_in, g_of, g_to, h_mask, gain, shift, out_bias, stat_tx, stat_rx, final_tx, final_rx, pick_own, pick_tx, pick_rx, mask,
    load_sem, send_sem, recv_sem, misc_tx, misc_rx, stat_sem_tx, stat_sem_rx, final_sem_tx, final_sem_rx, relay_rx, att_sem_tx, att_sem_rx, store_sem,
):
    clip = lax.axis_index("clip")
    space = lax.axis_index("space")
    core = clip % 2
    y = (clip // 2) % 2
    z = (clip // 4) % 4
    x = clip // 16
    chip = clip // 2

    def device(x, z, y, core):
        return (((x * 4 + z) * 2 + y) * 2 + core, space)

    def along(first, step):
        on_x = (1 - core) if first else core
        return device((x + step * on_x) % 4, (z + step * (1 - on_x)) % 4, y, core)

    a_up, a_down = along(True, 1), along(True, 3)
    b_up, b_down = along(False, 1), along(False, 3)
    y_pair = device(x, z, 1 - y, core)
    sibling = (clip + 1 - 2 * core, space)
    stats_to = [(clip, 1 - space), sibling, (clip + 1 - 2 * core, 1 - space)]
    edge_chip = (chip + 2 * core + 31) % 32
    edge_to = [(edge_chip * 2, space), (edge_chip * 2 + 1, space)]
    edge_from = [(((chip + 31) % 32) * 2 + 1, space), (((chip + 1) % 32) * 2, space)]

    relay_z = (z + 2 * y + 3) % 4
    relay_to = [device(x, relay_z, y, k) for k in range(2)]
    origin_z = (z + 5 - 2 * y) % 4
    relay_from = [device(x, origin_z, y, k) for k in range(2)]
    crossing = y * (1 - (z + 2) // 3) + (1 - y) * (z // 3)
    cross_to = device((x + 2 * y + 3) % 4, z, y, core)
    cross_from = device((x + 5 - 2 * y) % 4, z, y, core)

    edge_up = core * y * (1 - (z + 2) // 3)
    edge_down = core * (1 - y) * (z // 3)

    barrier = pltpu.get_barrier_semaphore()
    greet = [a_up, a_down, b_up, b_down, y_pair] + stats_to + edge_to + edge_from
    greet += relay_to + relay_from + [cross_to, cross_from]
    for other in greet:
        pl.semaphore_signal(barrier, inc=1, device_id=other, device_id_type=MESH)

    loads = [
        pltpu.make_async_copy(src, dst, load_sem.at[n])
        for n, (src, dst) in enumerate(
            [
                (latent, lat),
                (group_of, g_of),
                (group_to, g_to),
                (swap16, s16),
                (edge_out, e_out),
                (gain_in, gain),
                (shift_in, shift),
                (bias_in, out_bias),
                (wq, w.at[0]),
                (wk, w.at[1]),
                (wv, w.at[2]),
                (swap8, s8),
                (edge_in, e_in),
                (head_mask, h_mask),
                (wo, w_out),
            ]
        )
    ]
    for copy in loads[:8]:
        copy.start()

    row = lax.broadcasted_iota(jnp.int32, (48, 128), 0)
    lane = lax.broadcasted_iota(jnp.int32, (48, 128), 1)
    q_clip = (((lane >> 4) & 1) + core) & 1
    k_clip = (((row >> 4) & 1) + core) & 1
    frame = row & 15
    local = (row < 32) & (
        (k_clip == q_clip)
        | ((q_clip == 0) & (frame < EDGE))
        | ((q_clip == 1) & (frame >= FRAMES - EDGE))
    )
    left = (row >= 32) & (row < 36) & (q_clip == 0) & (chip > 0)
    right = (row >= 36) & (row < 40) & (q_clip == 1) & (chip < 31)
    mask[...] = jnp.where(local | left | right, 0.0, -jnp.inf).astype(F32)

    loads[0].wait()
    for copy in loads[8:]:
        copy.start()

    def add_rows(f, acc):
        v = lat[f].astype(F32)
        for r in range(ROWS // 8):
            acc = acc + v[8 * r : 8 * r + 8]
        return acc

    total = lax.fori_loop(0, FRAMES, add_rows, jnp.zeros((8, C), F32))
    loads[1].wait()
    loads[2].wait()
    count = FRAMES * ROWS * (C // GROUPS)
    mean_here = jnp.sum(exact_dot(total, g_of[...]), axis=0, keepdims=True) * (1.0 / count)
    mean_here = jnp.broadcast_to(mean_here, (8, 128))
    wide = exact_dot(mean_here, g_to[...])

    def add_squares(f, acc):
        v = lat[f].astype(F32)
        for r in range(ROWS // 8):
            d = v[8 * r : 8 * r + 8] - wide
            acc = acc + d * d
        return acc

    squares = lax.fori_loop(0, FRAMES, add_squares, jnp.zeros((8, C), F32))
    dev_here = jnp.sum(exact_dot(squares, g_of[...]), axis=0, keepdims=True)
    dev_here = jnp.broadcast_to(dev_here, (8, 128))
    first_row = lax.broadcasted_iota(jnp.int32, (8, 128), 0) == 0
    stat_tx[...] = jnp.where(first_row, mean_here, dev_here)

    picked = lat[picks[0, 0]].astype(F32)
    low, high = picked[:HALF], picked[HALF:]
    pick_own[...] = jnp.where(core == 0, low, high)
    pick_tx[...] = jnp.where(core == 0, high, low)

    pl.semaphore_wait(barrier, len(greet))

    def misc(n, src, dst, to):
        return pltpu.make_async_remote_copy(
            src_ref=src, dst_ref=dst, send_sem=misc_tx.at[n], recv_sem=misc_rx.at[n], device_id=to, device_id_type=MESH
        )

    stats = [
        pltpu.make_async_remote_copy(
            src_ref=stat_tx,
            dst_ref=stat_rx.at[n],
            send_sem=stat_sem_tx.at[n],
            recv_sem=stat_sem_rx.at[n],
            device_id=to,
            device_id_type=MESH,
        )
        for n, to in enumerate(stats_to)
    ]
    for copy in stats:
        copy.start()
    swap_pick = misc(1, pick_tx, pick_rx, sibling)
    swap_pick.start()

    loads[4].wait()
    edge_rows = lat[pl.ds(12 * core, EDGE)].reshape(EDGE * ROWS, C)
    edge_tx[...] = dot(e_out[...], edge_rows).astype(BF16).reshape(2, 96, C)
    relays = [
        pltpu.make_async_remote_copy(
            src_ref=edge_tx.at[k],
            dst_ref=edge_relay,
            send_sem=misc_tx.at[3 + k],
            recv_sem=relay_rx.at[0],
            device_id=relay_to[k],
            device_id_type=MESH,
        )
        for k in range(2)
    ]
    directs = [
        pltpu.make_async_remote_copy(
            src_ref=edge_tx.at[k],
            dst_ref=edge_rx.at[1 - core],
            send_sem=misc_tx.at[5 + k],
            recv_sem=misc_rx.at[3 + 1 - core],
            device_id=edge_to[k],
            device_id_type=MESH,
        )
        for k in range(2)
    ]
    cross = pltpu.make_async_remote_copy(
        src_ref=edge_relay,
        dst_ref=edge_cross,
        send_sem=misc_tx.at[8],
        recv_sem=relay_rx.at[1],
        device_id=cross_to,
        device_id_type=MESH,
    )

    def pass_along_y(src):
        return pltpu.make_async_remote_copy(
            src_ref=src,
            dst_ref=edge_rx.at[1 - y],
            send_sem=misc_tx.at[7],
            recv_sem=misc_rx.at[3 + 1 - y],
            device_id=y_pair,
            device_id_type=MESH,
        )

    @pl.when(core == y)
    def _():
        for copy in relays:
            copy.start()

    def send_edges():
        @pl.when(core != y)
        def _():
            for copy in directs:
                copy.start()

        @pl.when(crossing == 0)
        def _():
            pass_along_y(edge_relay).start()

    def send_crossed():
        @pl.when(crossing == 1)
        def _():
            cross.wait_recv()
            pass_along_y(edge_cross).start()

    loads[3].wait()
    for q in range(3):
        rows = lat[:, 16 * q : 16 * q + 16, :].reshape(256, C)
        turned[16 * q : 16 * q + 16] = dot(s16[...], rows).astype(BF16).reshape(16, 16, C)
    swap_rows = misc(2, turned.at[pl.ds(HALF * (1 - core), HALF)], sib, sibling)
    swap_rows.start()

    for copy in stats:
        copy.wait_recv()

    loads[5].wait()
    loads[6].wait()

    def combine(one, two):
        mean_one, mean_two = one[0:1], two[0:1]
        gap = mean_one - mean_two
        var = (one[1:2] + two[1:2] + gap * gap * (0.5 * count)) * (0.5 / count)
        return [0.5 * (mean_one + mean_two), lax.rsqrt(var + EPS)]

    table = combine(stat_tx[...], stat_rx[0]) + combine(stat_rx[1], stat_rx[2])
    final_tx[...] = jnp.concatenate(table + table, axis=0)
    final_sends = [
        pltpu.make_async_remote_copy(
            src_ref=final_tx,
            dst_ref=final_rx.at[1 - core],
            send_sem=final_sem_tx.at[k],
            recv_sem=final_sem_rx.at[1 - core],
            device_id=edge_to[k],
            device_id_type=MESH,
        )
        for k in range(2)
    ]
    for copy in final_sends:
        copy.start()
    table = exact_dot(final_tx[...], g_to[...])
    gains = gain[...].reshape(1, C)
    shifts = shift[...].reshape(1, C)

    def norm(v, sib_clip):
        at = 2 if sib_clip else 0
        return (v.astype(F32) - table[at : at + 1]) * (table[at + 1 : at + 2] * gains) + shifts

    swap_pick.wait_recv()
    for g in range(3):
        part = slice(8 * g, 8 * g + 8)
        pair = jnp.concatenate([norm(pick_own[part], False), norm(pick_rx[part], True)], axis=0)
        ctx[g, 0:16, :] = pair.astype(BF16)

    def leaves_down(i, s):
        if i < 2:
            return edge_up if s == 0 else 1 - edge_down
        return s

    def hop(i, j, s):
        if j == 0:
            if i == 0:
                src, to = (0, 0, 0), y_pair
            elif i == 1:
                src, to = (0, 0, s), a_up
            elif i == 2:
                src, to = (0, 0, s), a_down
            else:
                src, to = ((1, 0, 0), a_up) if s == 0 else ((2, 0, 1), a_down)
        elif j == 1:
            src, to = (i, 0, s), b_up
        elif j == 2:
            src, to = (i, 0, s), b_down
        else:
            down = leaves_down(i, s)
            src, to = (i, 1 + down, s), along(False, 1 + 2 * down)
        n, dst = slot_of(*src), slot_of(i, j, s)
        return pltpu.make_async_remote_copy(
            src_ref=ctx.at[:, pl.ds(pl.multiple_of(16 * n, 16), 16), :],
            dst_ref=ctx.at[:, 16 * dst : 16 * dst + 16, :],
            send_sem=send_sem.at[dst],
            recv_sem=recv_sem.at[dst],
            device_id=to,
            device_id_type=MESH,
        )

    def start(*slots):
        for slot in slots:
            hop(*slot).start()

    start((0, 0, 1), (1, 0, 0), (2, 0, 0), (0, 1, 0), (0, 2, 0))

    def edge_arrived(n):
        pltpu.make_async_copy(edge_rx.at[n], edge_rx.at[n], misc_rx.at[3 + n]).wait()
        pltpu.make_async_copy(final_rx.at[n], final_rx.at[n], final_sem_rx.at[n]).wait()

    def pass_on(arrived, *slots):
        def act():
            hop(*arrived).wait_recv()
            start(*slots)

        return act

    def arrive(i, j, s):
        n = slot_of(i, j, s)
        here = ctx.at[:, pl.ds(pl.multiple_of(16 * n, 16), 16), :]
        pltpu.make_async_copy(here, here, recv_sem.at[n]).wait()

    def forward(i, s):
        def act():
            arrive(i, 1 + leaves_down(i, s), s)
            start((i, 3, s))

        return act

    def project(rows, m):
        return dot(rows, w[m])

    def kv_steps(rows, store, *acts):
        def step(m, _):
            for n, act in enumerate(acts):
                pl.when(m == n)(act)
            store(m, project(rows(), 1 + m))
            return 0

        lax.fori_loop(0, 2, step, 0)

    def store_rows(at, n):
        def store(m, res):
            kv[m, :, at : at + n, :] = res.astype(BF16).reshape(HALF, n, C)

        return store

    def gather_ctx(j, at):
        for g in range(3):
            rows = dot(s8[...], ctx[g, 128 * j : 128 * j + 128, :]).astype(BF16)
            xc[8 * g : 8 * g + 8, at : at + 16, :] = rows.reshape(8, 16, C)

    def many(*acts):
        def act():
            for one in acts:
                one()

        return act

    own_x[:, 0:16, :] = norm(turned[pl.ds(HALF * core, HALF)], False).astype(BF16)
    swap_rows.wait_recv()
    own_x[:, 16:32, :] = norm(sib[...], True).astype(BF16)

    relays[0].wait_recv()

    @pl.when(crossing == 1)
    def _():
        cross.start()

    def own_rows():
        return own_x[...].reshape(HALF * 32, C)

    loads[8].wait()
    query[...] = (project(own_rows(), 0) * (HEAD_DIM**-0.5)).astype(BF16).reshape(HALF, 32, C)
    loads[9].wait()
    loads[10].wait()
    kv_steps(
        own_rows,
        store_rows(64, 32),
        many(
            pass_on((0, 0, 1), (1, 0, 1), (2, 0, 1), (0, 1, 1), (0, 2, 1)),
            pass_on((1, 0, 0), (3, 0, 0), (1, 1, 0), (1, 2, 0)),
            pass_on((2, 0, 0), (2, 1, 0), (2, 2, 0)),
            send_edges,
            forward(0, 0),
        ),
        many(
            pass_on((2, 0, 1), (3, 0, 1), (2, 1, 1), (2, 2, 1)),
            pass_on((1, 0, 1), (1, 1, 1), (1, 2, 1)),
        ),
    )
    pass_on((3, 0, 0), (3, 1, 0), (3, 2, 0))()
    forward(0, 1)()
    pass_on((3, 0, 1), (3, 1, 1), (3, 2, 1))()
    loads[11].wait()
    gather_ctx(0, 0)

    def one_phase():
        return xc[:, 0:16, :].reshape(HALF * 16, C)

    kv_steps(one_phase, store_rows(0, 16), many(forward(1, 0), send_crossed), many(forward(2, 0), forward(2, 1)))

    forward(1, 1)()
    forward(3, 0)()
    forward(3, 1)()
    for i in range(4):
        for s in range(2):
            arrive(i, 2 - leaves_down(i, s), s)
    gather_ctx(1, 0)
    gather_ctx(2, 16)
    kv_steps(lambda: xc[...].reshape(HALF * 32, C), store_rows(16, 32))
    loads[12].wait()
    edge_arrived(0)
    edge_arrived(1)
    left_side = lax.broadcasted_iota(jnp.int32, (8, C), 0) < EDGE
    left_table = exact_dot(final_rx[0], g_to[...])
    right_table = exact_dot(final_rx[1], g_to[...])
    edge_mean = jnp.where(left_side, left_table[0:1], right_table[0:1])
    edge_gain = jnp.where(left_side, left_table[1:2] * gains, right_table[1:2] * gains)
    rows = dot(e_in[...], edge_rx[...].reshape(192, C)).reshape(HALF, 8, C)
    edge_x[...] = ((rows - edge_mean) * edge_gain + shifts).astype(BF16).reshape(HALF * 8, C)

    def edge_rows_in():
        return edge_x[...]

    def store_edges(m, res):
        res = jnp.concatenate([res.reshape(HALF, 8, C), jnp.zeros((HALF, 8, C), F32)], axis=1)
        kv[m, :, 96:112, :] = res.astype(BF16)

    kv_steps(edge_rows_in, store_edges)

    for i in range(4):
        for s in range(2):
            hop(i, 3, s).wait_recv()
    gather_ctx(3, 0)
    kv_steps(one_phase, store_rows(48, 16))

    loads[13].wait()
    loads[14].wait()

    def send_att(c):
        there = pl.ds(HALF * core + 8 * c, 8)
        return pltpu.make_async_remote_copy(
            src_ref=att_tx.at[8 * c : 8 * c + 8],
            dst_ref=att.at[there],
            send_sem=att_sem_tx.at[c],
            recv_sem=att_sem_rx.at[c],
            device_id=sibling,
            device_id_type=MESH,
        )

    def attend(block, _):
        half = lax.broadcasted_iota(jnp.int32, (32, 128), 1) < HEAD_DIM
        units = [(block * 8 + n, h) for n in range(8) for h in range(TILES)]
        cols = [slice(h * TILE, (h + 1) * TILE) for h in range(TILES)]
        scores, weights, mixed = [], [], []
        for p, h in units:
            q = jnp.concatenate([query[p, :, cols[h]]] * 4, axis=0) * h_mask[...]
            scores.append(
                lax.dot_general(kv[0, p, :, cols[h]], q, (((1,), (1,)), ((), ())), preferred_element_type=F32)
            )
        for s in scores:
            s = jnp.concatenate([s[:64], s[64:] + mask[...]], axis=0)
            expo = jnp.exp(s - jnp.max(s, axis=0, keepdims=True))
            share = 1.0 / jnp.sum(expo, axis=0, keepdims=True)
            weights.append((expo * share).astype(BF16))
        for (p, h), s in zip(units, weights):
            mixed.append(
                lax.dot_general(s, kv[1, p, :, cols[h]], (((0,), (0,)), ((), ())), preferred_element_type=F32)
            )
        for (p, h), m in zip(units, mixed):
            for t in range(2):
                lanes = slice(128 * t, 128 * t + 128)
                both = jnp.where(half, m[64 * t : 64 * t + 32, lanes], m[64 * t + 32 : 64 * t + 64, lanes])
                both = both.astype(BF16)
                to = slice(h * TILE + 128 * t, h * TILE + 128 * t + 128)
                att[HALF * core + p, :, to] = both[:16]
                att_tx[p, :, to] = both[16:]
        return 0

    for c in range(3):
        lax.fori_loop(c, c + 1, attend, 0)
        send_att(c).start()

    def att_arrived(c):
        there = pl.ds(HALF * (1 - core) + 8 * c, 8)
        pltpu.make_async_copy(att.at[there], att.at[there], att_sem_rx.at[c]).wait()

    loads[7].wait()

    stores = []
    for t in range(3):
        if t == 1:
            att_arrived(0)
            att_arrived(1)
        elif t == 2:
            att_arrived(2)
        q = (t + 2 * core) % 3
        there = pl.ds(pl.multiple_of(q * 16, 16), 16)
        rows = dot(s16[...], att[there].reshape(256, C)).astype(BF16)
        res = dot(rows, w_out[...]).reshape(FRAMES, 16, C) + out_bias[...].reshape(1, 1, C)
        result[t] = (lat[:, there, :].astype(F32) + res).astype(BF16)
        stores.append(pltpu.make_async_copy(result.at[t], out.at[:, there, :], store_sem.at[t]))
        stores[t].start()

    for copy in stats:
        copy.wait_send()
    swap_pick.wait_send()
    swap_rows.wait_send()
    for copy in final_sends + [pass_along_y(edge_relay)]:
        copy.wait_send()

    @pl.when(crossing == 1)
    def _():
        cross.wait_send()

    @pl.when(core == y)
    def _():
        for copy in relays:
            copy.wait_send()

    @pl.when(core != y)
    def _():
        for copy in directs:
            copy.wait_send()

    for j in range(4):
        for i in range(4):
            for s in range(2):
                if (i, j, s) != (0, 0, 0):
                    hop(i, j, s).wait_send()
    for c in range(3):
        send_att(c).wait_send()
    for copy in stores:
        copy.wait()


def local(latent, gn_gain, gn_bias, w_query, w_key, w_value, w_out, out_bias, context_frames):
    consts = [
        jnp.asarray(SWAP16, BF16),
        jnp.asarray(SWAP8, BF16),
        jnp.asarray(EDGE_OUT, BF16),
        jnp.asarray(EDGE_IN, BF16),
        jnp.asarray(GROUP_OF, BF16),
        jnp.asarray(GROUP_OF.T.copy(), BF16),
        jnp.asarray(HEAD_MASK, BF16),
    ]
    any_ = pl.BlockSpec(memory_space=pl.ANY)
    smem = pl.BlockSpec(memory_space=pltpu.SMEM)
    dma = pltpu.SemaphoreType.DMA
    return pl.pallas_call(
        kernel,
        out_shape=jax.ShapeDtypeStruct((FRAMES, ROWS, C), BF16),
        in_specs=[any_] * 8 + [smem] + [any_] * 7,
        out_specs=any_,
        scratch_shapes=[
            pltpu.VMEM((FRAMES, ROWS, C), BF16),
            pltpu.VMEM((ROWS, FRAMES, C), BF16),
            pltpu.VMEM((HALF, FRAMES, C), BF16),
            pltpu.VMEM((HALF, 32, C), BF16),
            pltpu.VMEM((3, 512, C), BF16),
            pltpu.VMEM((HALF, 32, C), BF16),
            pltpu.VMEM((2, 96, C), BF16),
            pltpu.VMEM((96, C), BF16),
            pltpu.VMEM((96, C), BF16),
            pltpu.VMEM((2, 96, C), BF16),
            pltpu.VMEM((192, C), BF16),
            pltpu.VMEM((HALF, 32, C), BF16),
            pltpu.VMEM((2, HALF, KEYS, C), BF16),
            pltpu.VMEM((ROWS, FRAMES, C), BF16),
            pltpu.VMEM((HALF, FRAMES, C), BF16),
            pltpu.VMEM((3, FRAMES, 16, C), BF16),
            pltpu.VMEM((3, C, C), BF16),
            pltpu.VMEM((C, C), BF16),
            pltpu.VMEM((256, 256), BF16),
            pltpu.VMEM((128, 128), BF16),
            pltpu.VMEM((192, 192), BF16),
            pltpu.VMEM((192, 192), BF16),
            pltpu.VMEM((C, 128), BF16),
            pltpu.VMEM((128, C), BF16),
            pltpu.VMEM((128, TILE), BF16),
            pltpu.VMEM((C,), F32),
            pltpu.VMEM((C,), F32),
            pltpu.VMEM((C,), F32),
            pltpu.VMEM((8, 128), F32),
            pltpu.VMEM((3, 8, 128), F32),
            pltpu.VMEM((8, 128), F32),
            pltpu.VMEM((2, 8, 128), F32),
            pltpu.VMEM((HALF, C), F32),
            pltpu.VMEM((HALF, C), F32),
            pltpu.VMEM((HALF, C), F32),
            pltpu.VMEM((48, 128), F32),
            dma((15,)),
            dma((32,)),
            dma((32,)),
            dma((9,)),
            dma((5,)),
            dma((3,)),
            dma((3,)),
            dma((2,)),
            dma((2,)),
            dma((2,)),
            dma((3,)),
            dma((3,)),
            dma((3,)),
        ],
        compiler_params=pltpu.CompilerParams(
            collective_id=0, has_side_effects=True, vmem_limit_bytes=60 * 1024 * 1024
        ),
        cost_estimate=pl.CostEstimate(flops=25 * 10**9, bytes_accessed=18 * 10**6, transcendentals=2 * 10**6),
    )(
        latent, gn_gain, gn_bias, w_query, w_key, w_value, w_out,
        out_bias, context_frames, *consts,
    )


def solution(mesh):
    placed = (P("clip", "space", None), P(), P(), P(), P(), P(), P(), P(), P("clip", None))
    return jax.shard_map(
        local, mesh=mesh, in_specs=placed, out_specs=P("clip", "space", None), check_vma=False
    )
```

```python
import numpy as np

import jax
import jax.numpy as jnp
from jax import lax
from jax.experimental import pallas as pl
from jax.experimental.pallas import tpu as pltpu
from jax.sharding import PartitionSpec as P

C = 1280
HEAD_DIM = 64
GROUPS = 32
FRAMES = 16
EDGE = 4
EPS = 1e-06
ROWS = 48
HALF = 24
KEYS = 112
TILE = 256
TILES = C // TILE
MESH = pl.DeviceIdType.MESH
F32, BF16 = jnp.float32, jnp.bfloat16


def swap_matrix(outer, inner, blocks=1):
    n = outer * inner
    m = np.zeros((n, n), np.float32)
    for i in range(outer):
        for j in range(inner):
            m[j * outer + i, i * inner + j] = 1
    return m


def edge_merge():
    m = np.zeros((192, 192), np.float32)
    for side in range(2):
        for p in range(HALF):
            for f in range(EDGE):
                m[p * 8 + side * 4 + f, side * 96 + p * 4 + f] = 1
    return m


SWAP16 = swap_matrix(16, 16)
SWAP8 = swap_matrix(16, 8)
EDGE_OUT = swap_matrix(EDGE, ROWS)
EDGE_IN = edge_merge()
GROUP_OF = np.zeros((C, 128), np.float32)
GROUP_OF[np.arange(C), np.arange(C) // (C // GROUPS)] = 1
HEAD_MASK = np.zeros((128, TILE), np.float32)
for _h in range(4):
    HEAD_MASK[_h * 32 : _h * 32 + 32, _h * 64 : _h * 64 + 64] = 1


def dot(a, b):
    return jnp.dot(a, b, preferred_element_type=F32)


def exact_dot(a, b):
    high = a.astype(BF16).astype(F32)
    mid = (a - high).astype(BF16).astype(F32)
    low = a - high - mid
    n = a.shape[0]
    res = dot(jnp.concatenate([high, mid, low], axis=0).astype(BF16), b)
    return res[:n] + res[n : 2 * n] + res[2 * n :]


def slot_of(i, j, s):
    return j * 8 + i * 2 + s


def kernel(
    latent, gain_in, shift_in, wq, wk, wv, wo, bias_in, picks, swap16, swap8, edge_out, edge_in, group_of, group_to, head_mask,
    out,
    lat, turned, sib, own_x, ctx, xc, edge_tx, edge_relay, edge_cross, edge_rx, edge_x, query, kv, att, att_tx, result, w, w_out,
    s16, s8, e_out, e_in, g_of, g_to, h_mask, gain, shift, out_bias, stat_tx, stat_rx, final_tx, final_rx, pick_own, pick_tx, pick_rx, mask,
    load_sem, send_sem, recv_sem, misc_tx, misc_rx, stat_sem_tx, stat_sem_rx, final_sem_tx, final_sem_rx, relay_rx, att_sem_tx, att_sem_rx, store_sem,
):
    clip = lax.axis_index("clip")
    space = lax.axis_index("space")
    core = clip % 2
    y = (clip // 2) % 2
    z = (clip // 4) % 4
    x = clip // 16
    chip = clip // 2

    def device(x, z, y, core):
        return (((x * 4 + z) * 2 + y) * 2 + core, space)

    def along(first, step):
        on_x = (1 - core) if first else core
        return device((x + step * on_x) % 4, (z + step * (1 - on_x)) % 4, y, core)

    a_up, a_down = along(True, 1), along(True, 3)
    b_up, b_down = along(False, 1), along(False, 3)
    y_pair = device(x, z, 1 - y, core)
    sibling = (clip + 1 - 2 * core, space)
    stats_to = [(clip, 1 - space), sibling, (clip + 1 - 2 * core, 1 - space)]
    edge_chip = (chip + 2 * core + 31) % 32
    edge_to = [(edge_chip * 2, space), (edge_chip * 2 + 1, space)]
    edge_from = [(((chip + 31) % 32) * 2 + 1, space), (((chip + 1) % 32) * 2, space)]

    relay_z = (z + 2 * y + 3) % 4
    relay_to = [device(x, relay_z, y, k) for k in range(2)]
    origin_z = (z + 5 - 2 * y) % 4
    relay_from = [device(x, origin_z, y, k) for k in range(2)]
    crossing = y * (1 - (z + 2) // 3) + (1 - y) * (z // 3)
    cross_to = device((x + 2 * y + 3) % 4, z, y, core)
    cross_from = device((x + 5 - 2 * y) % 4, z, y, core)

    edge_up = core * y * (1 - (z + 2) // 3)
    edge_down = core * (1 - y) * (z // 3)

    barrier = pltpu.get_barrier_semaphore()
    greet = [a_up, a_down, b_up, b_down, y_pair] + stats_to + edge_to + edge_from
    greet += relay_to + relay_from + [cross_to, cross_from]
    for other in greet:
        pl.semaphore_signal(barrier, inc=1, device_id=other, device_id_type=MESH)

    loads = [
        pltpu.make_async_copy(src, dst, load_sem.at[n])
        for n, (src, dst) in enumerate(
            [
                (latent, lat),
                (group_of, g_of),
                (group_to, g_to),
                (swap16, s16),
                (edge_out, e_out),
                (gain_in, gain),
                (shift_in, shift),
                (bias_in, out_bias),
                (wq, w.at[0]),
                (wk, w.at[1]),
                (wv, w.at[2]),
                (swap8, s8),
                (edge_in, e_in),
                (head_mask, h_mask),
                (wo, w_out),
            ]
        )
    ]
    for copy in loads[:8]:
        copy.start()

    row = lax.broadcasted_iota(jnp.int32, (48, 128), 0)
    lane = lax.broadcasted_iota(jnp.int32, (48, 128), 1)
    q_clip = (((lane >> 4) & 1) + core) & 1
    k_clip = (((row >> 4) & 1) + core) & 1
    frame = row & 15
    local = (row < 32) & (
        (k_clip == q_clip)
        | ((q_clip == 0) & (frame < EDGE))
        | ((q_clip == 1) & (frame >= FRAMES - EDGE))
    )
    left = (row >= 32) & (row < 36) & (q_clip == 0) & (chip > 0)
    right = (row >= 36) & (row < 40) & (q_clip == 1) & (chip < 31)
    mask[...] = jnp.where(local | left | right, 0.0, -jnp.inf).astype(F32)

    loads[0].wait()
    for copy in loads[8:]:
        copy.start()

    def fold(v):
        acc = v[:8]
        for r in range(1, ROWS // 8):
            acc = acc + v[8 * r : 8 * r + 8]
        return acc

    loads[1].wait()
    loads[2].wait()
    count = FRAMES * ROWS * (C // GROUPS)
    about = jnp.sum(exact_dot(fold(lat[0].astype(F32)), g_of[...]), axis=0, keepdims=True) * (FRAMES / count)
    wide = exact_dot(jnp.broadcast_to(about, (8, 128)), g_to[...])[0:1]

    def add_frame(f, acc):
        d = lat[f].astype(F32) - wide
        return acc[0] + fold(d), acc[1] + fold(d * d)

    zero = jnp.zeros((8, C), F32)
    sums = exact_dot(jnp.concatenate(lax.fori_loop(0, FRAMES, add_frame, (zero, zero)), axis=0), g_of[...])
    shift_sum = jnp.sum(sums[:8], axis=0, keepdims=True)
    square_sum = jnp.sum(sums[8:], axis=0, keepdims=True)
    mean_here = jnp.broadcast_to(about + shift_sum * (1.0 / count), (8, 128))
    dev_here = jnp.maximum(square_sum - shift_sum * shift_sum * (1.0 / count), 0.0)
    dev_here = jnp.broadcast_to(dev_here, (8, 128))
    first_row = lax.broadcasted_iota(jnp.int32, (8, 128), 0) == 0
    stat_tx[...] = jnp.where(first_row, mean_here, dev_here)

    picked = lat[picks[0, 0]].astype(F32)
    low, high = picked[:HALF], picked[HALF:]
    pick_own[...] = jnp.where(core == 0, low, high)
    pick_tx[...] = jnp.where(core == 0, high, low)

    pl.semaphore_wait(barrier, len(greet))

    def misc(n, src, dst, to):
        return pltpu.make_async_remote_copy(
            src_ref=src, dst_ref=dst, send_sem=misc_tx.at[n], recv_sem=misc_rx.at[n], device_id=to, device_id_type=MESH
        )

    stats = [
        pltpu.make_async_remote_copy(
            src_ref=stat_tx,
            dst_ref=stat_rx.at[n],
            send_sem=stat_sem_tx.at[n],
            recv_sem=stat_sem_rx.at[n],
            device_id=to,
            device_id_type=MESH,
        )
        for n, to in enumerate(stats_to)
    ]
    for copy in stats:
        copy.start()
    swap_pick = misc(1, pick_tx, pick_rx, sibling)
    swap_pick.start()

    loads[4].wait()
    edge_rows = lat[pl.ds(12 * core, EDGE)].reshape(EDGE * ROWS, C)
    edge_tx[...] = dot(e_out[...], edge_rows).astype(BF16).reshape(2, 96, C)
    relays = [
        pltpu.make_async_remote_copy(
            src_ref=edge_tx.at[k],
            dst_ref=edge_relay,
            send_sem=misc_tx.at[3 + k],
            recv_sem=relay_rx.at[0],
            device_id=relay_to[k],
            device_id_type=MESH,
        )
        for k in range(2)
    ]
    directs = [
        pltpu.make_async_remote_copy(
            src_ref=edge_tx.at[k],
            dst_ref=edge_rx.at[1 - core],
            send_sem=misc_tx.at[5 + k],
            recv_sem=misc_rx.at[3 + 1 - core],
            device_id=edge_to[k],
            device_id_type=MESH,
        )
        for k in range(2)
    ]
    cross = pltpu.make_async_remote_copy(
        src_ref=edge_relay,
        dst_ref=edge_cross,
        send_sem=misc_tx.at[8],
        recv_sem=relay_rx.at[1],
        device_id=cross_to,
        device_id_type=MESH,
    )

    def pass_along_y(src):
        return pltpu.make_async_remote_copy(
            src_ref=src,
            dst_ref=edge_rx.at[1 - y],
            send_sem=misc_tx.at[7],
            recv_sem=misc_rx.at[3 + 1 - y],
            device_id=y_pair,
            device_id_type=MESH,
        )

    @pl.when(core == y)
    def _():
        for copy in relays:
            copy.start()

    def send_edges():
        @pl.when(core != y)
        def _():
            for copy in directs:
                copy.start()

        @pl.when(crossing == 0)
        def _():
            pass_along_y(edge_relay).start()

    def send_crossed():
        @pl.when(crossing == 1)
        def _():
            cross.wait_recv()
            pass_along_y(edge_cross).start()

    loads[3].wait()
    for q in range(3):
        rows = lat[:, 16 * q : 16 * q + 16, :].reshape(256, C)
        turned[16 * q : 16 * q + 16] = dot(s16[...], rows).astype(BF16).reshape(16, 16, C)
    swap_rows = misc(2, turned.at[pl.ds(HALF * (1 - core), HALF)], sib, sibling)
    swap_rows.start()

    for copy in stats:
        copy.wait_recv()

    loads[5].wait()
    loads[6].wait()

    def combine(one, two):
        mean_one, mean_two = one[0:1], two[0:1]
        gap = mean_one - mean_two
        var = (one[1:2] + two[1:2] + gap * gap * (0.5 * count)) * (0.5 / count)
        return [0.5 * (mean_one + mean_two), lax.rsqrt(var + EPS)]

    table = combine(stat_tx[...], stat_rx[0]) + combine(stat_rx[1], stat_rx[2])
    final_tx[...] = jnp.concatenate(table + table, axis=0)
    final_sends = [
        pltpu.make_async_remote_copy(
            src_ref=final_tx,
            dst_ref=final_rx.at[1 - core],
            send_sem=final_sem_tx.at[k],
            recv_sem=final_sem_rx.at[1 - core],
            device_id=edge_to[k],
            device_id_type=MESH,
        )
        for k in range(2)
    ]
    for copy in final_sends:
        copy.start()
    table = exact_dot(final_tx[...], g_to[...])
    gains = gain[...].reshape(1, C)
    shifts = shift[...].reshape(1, C)

    def norm(v, sib_clip):
        at = 2 if sib_clip else 0
        return (v.astype(F32) - table[at : at + 1]) * (table[at + 1 : at + 2] * gains) + shifts

    swap_pick.wait_recv()
    for g in range(3):
        part = slice(8 * g, 8 * g + 8)
        pair = jnp.concatenate([norm(pick_own[part], False), norm(pick_rx[part], True)], axis=0)
        ctx[g, 0:16, :] = pair.astype(BF16)

    def leaves_down(i, s):
        if i < 2:
            return edge_up if s == 0 else 1 - edge_down
        return s

    def hop(i, j, s):
        if j == 0:
            if i == 0:
                src, to = (0, 0, 0), y_pair
            elif i == 1:
                src, to = (0, 0, s), a_up
            elif i == 2:
                src, to = (0, 0, s), a_down
            else:
                src, to = ((1, 0, 0), a_up) if s == 0 else ((2, 0, 1), a_down)
        elif j == 1:
            src, to = (i, 0, s), b_up
        elif j == 2:
            src, to = (i, 0, s), b_down
        else:
            down = leaves_down(i, s)
            src, to = (i, 1 + down, s), along(False, 1 + 2 * down)
        n, dst = slot_of(*src), slot_of(i, j, s)
        return pltpu.make_async_remote_copy(
            src_ref=ctx.at[:, pl.ds(pl.multiple_of(16 * n, 16), 16), :],
            dst_ref=ctx.at[:, 16 * dst : 16 * dst + 16, :],
            send_sem=send_sem.at[dst],
            recv_sem=recv_sem.at[dst],
            device_id=to,
            device_id_type=MESH,
        )

    def start(*slots):
        for slot in slots:
            hop(*slot).start()

    start((0, 0, 1), (1, 0, 0), (2, 0, 0), (0, 1, 0), (0, 2, 0))

    def edge_arrived(n):
        pltpu.make_async_copy(edge_rx.at[n], edge_rx.at[n], misc_rx.at[3 + n]).wait()
        pltpu.make_async_copy(final_rx.at[n], final_rx.at[n], final_sem_rx.at[n]).wait()

    def pass_on(arrived, *slots):
        def act():
            hop(*arrived).wait_recv()
            start(*slots)

        return act

    def arrive(i, j, s):
        n = slot_of(i, j, s)
        here = ctx.at[:, pl.ds(pl.multiple_of(16 * n, 16), 16), :]
        pltpu.make_async_copy(here, here, recv_sem.at[n]).wait()

    def forward(i, s):
        def act():
            arrive(i, 1 + leaves_down(i, s), s)
            start((i, 3, s))

        return act

    def project(rows, m):
        return dot(rows, w[m])

    def kv_steps(rows, store, *acts):
        def step(m, _):
            for n, act in enumerate(acts):
                pl.when(m == n)(act)
            store(m, project(rows(), 1 + m))
            return 0

        lax.fori_loop(0, 2, step, 0)

    def store_rows(at, n):
        def store(m, res):
            kv[m, :, at : at + n, :] = res.astype(BF16).reshape(HALF, n, C)

        return store

    def gather_ctx(j, at):
        for g in range(3):
            rows = dot(s8[...], ctx[g, 128 * j : 128 * j + 128, :]).astype(BF16)
            xc[8 * g : 8 * g + 8, at : at + 16, :] = rows.reshape(8, 16, C)

    def many(*acts):
        def act():
            for one in acts:
                one()

        return act

    own_x[:, 0:16, :] = norm(turned[pl.ds(HALF * core, HALF)], False).astype(BF16)
    swap_rows.wait_recv()
    own_x[:, 16:32, :] = norm(sib[...], True).astype(BF16)

    relays[0].wait_recv()

    @pl.when(crossing == 1)
    def _():
        cross.start()

    def own_rows():
        return own_x[...].reshape(HALF * 32, C)

    loads[8].wait()
    query[...] = (project(own_rows(), 0) * (HEAD_DIM**-0.5)).astype(BF16).reshape(HALF, 32, C)
    loads[9].wait()
    loads[10].wait()
    kv_steps(
        own_rows,
        store_rows(64, 32),
        many(
            pass_on((0, 0, 1), (1, 0, 1), (2, 0, 1), (0, 1, 1), (0, 2, 1)),
            pass_on((1, 0, 0), (3, 0, 0), (1, 1, 0), (1, 2, 0)),
            pass_on((2, 0, 0), (2, 1, 0), (2, 2, 0)),
            send_edges,
            forward(0, 0),
        ),
        many(
            pass_on((2, 0, 1), (3, 0, 1), (2, 1, 1), (2, 2, 1)),
            pass_on((1, 0, 1), (1, 1, 1), (1, 2, 1)),
        ),
    )
    pass_on((3, 0, 0), (3, 1, 0), (3, 2, 0))()
    forward(0, 1)()
    pass_on((3, 0, 1), (3, 1, 1), (3, 2, 1))()
    loads[11].wait()
    gather_ctx(0, 0)

    def one_phase():
        return xc[:, 0:16, :].reshape(HALF * 16, C)

    kv_steps(one_phase, store_rows(0, 16), many(forward(1, 0), send_crossed), many(forward(2, 0), forward(2, 1)))

    forward(1, 1)()
    forward(3, 0)()
    forward(3, 1)()
    for i in range(4):
        for s in range(2):
            arrive(i, 2 - leaves_down(i, s), s)
    gather_ctx(1, 0)
    gather_ctx(2, 16)
    kv_steps(lambda: xc[...].reshape(HALF * 32, C), store_rows(16, 32))
    loads[12].wait()
    edge_arrived(0)
    edge_arrived(1)
    left_side = lax.broadcasted_iota(jnp.int32, (8, C), 0) < EDGE
    left_table = exact_dot(final_rx[0], g_to[...])
    right_table = exact_dot(final_rx[1], g_to[...])
    edge_mean = jnp.where(left_side, left_table[0:1], right_table[0:1])
    edge_gain = jnp.where(left_side, left_table[1:2] * gains, right_table[1:2] * gains)
    rows = dot(e_in[...], edge_rx[...].reshape(192, C)).reshape(HALF, 8, C)
    edge_x[...] = ((rows - edge_mean) * edge_gain + shifts).astype(BF16).reshape(HALF * 8, C)

    def edge_rows_in():
        return edge_x[...]

    def store_edges(m, res):
        res = jnp.concatenate([res.reshape(HALF, 8, C), jnp.zeros((HALF, 8, C), F32)], axis=1)
        kv[m, :, 96:112, :] = res.astype(BF16)

    kv_steps(edge_rows_in, store_edges)

    for i in range(4):
        for s in range(2):
            hop(i, 3, s).wait_recv()
    gather_ctx(3, 0)
    kv_steps(one_phase, store_rows(48, 16))

    loads[13].wait()
    loads[14].wait()

    def send_att(c):
        there = pl.ds(HALF * core + 8 * c, 8)
        return pltpu.make_async_remote_copy(
            src_ref=att_tx.at[8 * c : 8 * c + 8],
            dst_ref=att.at[there],
            send_sem=att_sem_tx.at[c],
            recv_sem=att_sem_rx.at[c],
            device_id=sibling,
            device_id_type=MESH,
        )

    def attend(block, _):
        half = lax.broadcasted_iota(jnp.int32, (32, 128), 1) < HEAD_DIM
        units = [(block * 8 + n, h) for n in range(8) for h in range(TILES)]
        cols = [slice(h * TILE, (h + 1) * TILE) for h in range(TILES)]
        scores, weights, mixed = [], [], []
        for p, h in units:
            q = jnp.concatenate([query[p, :, cols[h]]] * 4, axis=0) * h_mask[...]
            scores.append(
                lax.dot_general(kv[0, p, :, cols[h]], q, (((1,), (1,)), ((), ())), preferred_element_type=F32)
            )
        for s in scores:
            s = jnp.concatenate([s[:64], s[64:] + mask[...]], axis=0)
            expo = jnp.exp(s - jnp.max(s, axis=0, keepdims=True))
            share = 1.0 / jnp.sum(expo, axis=0, keepdims=True)
            weights.append((expo * share).astype(BF16))
        for (p, h), s in zip(units, weights):
            mixed.append(
                lax.dot_general(s, kv[1, p, :, cols[h]], (((0,), (0,)), ((), ())), preferred_element_type=F32)
            )
        for (p, h), m in zip(units, mixed):
            for t in range(2):
                lanes = slice(128 * t, 128 * t + 128)
                both = jnp.where(half, m[64 * t : 64 * t + 32, lanes], m[64 * t + 32 : 64 * t + 64, lanes])
                both = both.astype(BF16)
                to = slice(h * TILE + 128 * t, h * TILE + 128 * t + 128)
                att[HALF * core + p, :, to] = both[:16]
                att_tx[p, :, to] = both[16:]
        return 0

    for c in range(3):
        lax.fori_loop(c, c + 1, attend, 0)
        send_att(c).start()

    def att_arrived(c):
        there = pl.ds(HALF * (1 - core) + 8 * c, 8)
        pltpu.make_async_copy(att.at[there], att.at[there], att_sem_rx.at[c]).wait()

    loads[7].wait()

    stores = []
    for t in range(3):
        if t == 1:
            att_arrived(0)
            att_arrived(1)
        elif t == 2:
            att_arrived(2)
        q = (t + 2 * core) % 3
        there = pl.ds(pl.multiple_of(q * 16, 16), 16)
        rows = dot(s16[...], att[there].reshape(256, C)).astype(BF16)
        res = dot(rows, w_out[...]).reshape(FRAMES, 16, C) + out_bias[...].reshape(1, 1, C)
        result[t] = (lat[:, there, :].astype(F32) + res).astype(BF16)
        stores.append(pltpu.make_async_copy(result.at[t], out.at[:, there, :], store_sem.at[t]))
        stores[t].start()

    for copy in stats:
        copy.wait_send()
    swap_pick.wait_send()
    swap_rows.wait_send()
    for copy in final_sends + [pass_along_y(edge_relay)]:
        copy.wait_send()

    @pl.when(crossing == 1)
    def _():
        cross.wait_send()

    @pl.when(core == y)
    def _():
        for copy in relays:
            copy.wait_send()

    @pl.when(core != y)
    def _():
        for copy in directs:
            copy.wait_send()

    for j in range(4):
        for i in range(4):
            for s in range(2):
                if (i, j, s) != (0, 0, 0):
                    hop(i, j, s).wait_send()
    for c in range(3):
        send_att(c).wait_send()
    for copy in stores:
        copy.wait()


def local(latent, gn_gain, gn_bias, w_query, w_key, w_value, w_out, out_bias, context_frames):
    consts = [
        jnp.asarray(SWAP16, BF16),
        jnp.asarray(SWAP8, BF16),
        jnp.asarray(EDGE_OUT, BF16),
        jnp.asarray(EDGE_IN, BF16),
        jnp.asarray(GROUP_OF, BF16),
        jnp.asarray(GROUP_OF.T.copy(), BF16),
        jnp.asarray(HEAD_MASK, BF16),
    ]
    any_ = pl.BlockSpec(memory_space=pl.ANY)
    smem = pl.BlockSpec(memory_space=pltpu.SMEM)
    dma = pltpu.SemaphoreType.DMA
    return pl.pallas_call(
        kernel,
        out_shape=jax.ShapeDtypeStruct((FRAMES, ROWS, C), BF16),
        in_specs=[any_] * 8 + [smem] + [any_] * 7,
        out_specs=any_,
        scratch_shapes=[
            pltpu.VMEM((FRAMES, ROWS, C), BF16),
            pltpu.VMEM((ROWS, FRAMES, C), BF16),
            pltpu.VMEM((HALF, FRAMES, C), BF16),
            pltpu.VMEM((HALF, 32, C), BF16),
            pltpu.VMEM((3, 512, C), BF16),
            pltpu.VMEM((HALF, 32, C), BF16),
            pltpu.VMEM((2, 96, C), BF16),
            pltpu.VMEM((96, C), BF16),
            pltpu.VMEM((96, C), BF16),
            pltpu.VMEM((2, 96, C), BF16),
            pltpu.VMEM((192, C), BF16),
            pltpu.VMEM((HALF, 32, C), BF16),
            pltpu.VMEM((2, HALF, KEYS, C), BF16),
            pltpu.VMEM((ROWS, FRAMES, C), BF16),
            pltpu.VMEM((HALF, FRAMES, C), BF16),
            pltpu.VMEM((3, FRAMES, 16, C), BF16),
            pltpu.VMEM((3, C, C), BF16),
            pltpu.VMEM((C, C), BF16),
            pltpu.VMEM((256, 256), BF16),
            pltpu.VMEM((128, 128), BF16),
            pltpu.VMEM((192, 192), BF16),
            pltpu.VMEM((192, 192), BF16),
            pltpu.VMEM((C, 128), BF16),
            pltpu.VMEM((128, C), BF16),
            pltpu.VMEM((128, TILE), BF16),
            pltpu.VMEM((C,), F32),
            pltpu.VMEM((C,), F32),
            pltpu.VMEM((C,), F32),
            pltpu.VMEM((8, 128), F32),
            pltpu.VMEM((3, 8, 128), F32),
            pltpu.VMEM((8, 128), F32),
            pltpu.VMEM((2, 8, 128), F32),
            pltpu.VMEM((HALF, C), F32),
            pltpu.VMEM((HALF, C), F32),
            pltpu.VMEM((HALF, C), F32),
            pltpu.VMEM((48, 128), F32),
            dma((15,)),
            dma((32,)),
            dma((32,)),
            dma((9,)),
            dma((5,)),
            dma((3,)),
            dma((3,)),
            dma((2,)),
            dma((2,)),
            dma((2,)),
            dma((3,)),
            dma((3,)),
            dma((3,)),
        ],
        compiler_params=pltpu.CompilerParams(
            collective_id=0, has_side_effects=True, vmem_limit_bytes=60 * 1024 * 1024
        ),
        cost_estimate=pl.CostEstimate(flops=25 * 10**9, bytes_accessed=18 * 10**6, transcendentals=2 * 10**6),
    )(
        latent, gn_gain, gn_bias, w_query, w_key, w_value, w_out,
        out_bias, context_frames, *consts,
    )


def solution(mesh):
    placed = (P("clip", "space", None), P(), P(), P(), P(), P(), P(), P(), P("clip", None))
    return jax.shard_map(
        local, mesh=mesh, in_specs=placed, out_specs=P("clip", "space", None), check_vma=False
    )
```
